256 devices in a mesh: grp: 2 (over x_lo), ctx: 16 (over z, x_hi), tp: 8 (over y, core).
Axes of the slice: x: 4 (x_hi: 2, x_lo: 2; x = x_hi * 2 + x_lo), y: 4, z: 8, core: 2. Of those that a mesh axis runs over, the one named last changes fastest.
Arguments:
- key_value_cache: bfloat16 [2, 32, 3072, 2048], P('grp', 'ctx', None, 'tp'), may hold values from -6 to 6
- new_kv: bfloat16 [2, 32, 2048], P('grp', 'ctx', 'tp'), may hold values from -6 to 6
- final_query: bfloat16 [2, 32, 8192], P('grp', 'ctx', 'tp'), may hold values from -484 to 484
- out_weight: bfloat16 [2, 8192, 2560], P('grp', 'tp'), may hold values from -0.25 to 0.25
- lengths: int32 [32], replicated, may hold values from 1 to 3072, as said below
- block_plan: int32 [192], replicated, may hold values from 0 to 15, as said below
- queries: bfloat16 [2, 3072, 8192], P('grp', 'ctx', 'tp'), may hold values from -480 to 480
- output_gradient: bfloat16 [2, 3072, 8192], P('grp', 'ctx', 'tp'), may hold values from -6 to 6
Outputs:
- decoded: bfloat16 [2, 32, 2560], P('grp', 'ctx')
- attn_out: bfloat16 [2, 3072, 8192], P('grp', 'ctx', 'tp')
- grad_query: bfloat16 [2, 3072, 8192], P('grp', 'ctx', 'tp')
- grad_kv: bfloat16 [2, 3072, 2048], P('grp', 'ctx', 'tp')
The draws below stay inside these ranges and needn't reach their ends.
Inputs may be any that keep to these rules, and one draw needn't show every extreme that they name: `lengths`: exactly one row has length 3072. `block_plan`: each shard number is given to exactly 12 blocks.
All inputs are finite; a program needn't handle non-finite values.
Results may differ from the reference program's by a relative error of at most 0.024.
Values may be sent and summed in bfloat16 or wider, within the bound.
No kernel may reach another device: no remote copies, remote signals or barrier semaphores. Data moves between devices by JAX's collectives and lax.ppermute only.
A program may use at most 128 MiB of HBM per device.

```python
import jax
import jax.numpy as jnp
from jax import lax

QUERY_HEADS = 64
KEY_VALUE_HEADS = 8
HEAD_SIZE = 128
DW = 2560
BLK = 16
BPD = 12
MAX_LENGTH = 3072
NBLK = 192
RESPONSE_ROWS = 32
GROUP_COUNT = 2


def shared_pairs(key):
    return jnp.clip(jax.random.normal(key, (GROUP_COUNT, RESPONSE_ROWS, 2 * KEY_VALUE_HEADS * HEAD_SIZE), jnp.float32), -6.0, 6.0)


def draw_new_kv(key, part):
    return shared_pairs(key).astype(jnp.bfloat16)


def draw_final_query(key, part):
    every_pair = shared_pairs(key)
    key = jax.random.fold_in(key, 11)
    response_keys = every_pair.reshape(GROUP_COUNT, RESPONSE_ROWS, KEY_VALUE_HEADS, 2, HEAD_SIZE)[:, :, :, 0, :]
    lifted_rows = jnp.broadcast_to(response_keys[:, :, :, None, :], (GROUP_COUNT, RESPONSE_ROWS, KEY_VALUE_HEADS, QUERY_HEADS // KEY_VALUE_HEADS, HEAD_SIZE)).reshape(GROUP_COUNT, RESPONSE_ROWS, QUERY_HEADS * HEAD_SIZE)
    noise_rows = jnp.clip(jax.random.normal(key, (GROUP_COUNT, RESPONSE_ROWS, QUERY_HEADS * HEAD_SIZE), jnp.float32), -6.0, 6.0)
    return (noise_rows + 0.6 * lifted_rows).astype(jnp.bfloat16)


def draw_queries(key, part):
    key = jax.random.fold_in(key, 23)
    noise_rows = jnp.clip(jax.random.normal(key, (GROUP_COUNT, MAX_LENGTH, QUERY_HEADS * HEAD_SIZE), jnp.float32), -6.0, 6.0)
    return noise_rows.astype(jnp.bfloat16)


def draw_lengths(key, part):
    key = jax.random.fold_in(key, 31)
    base_lengths = jax.random.randint(key, (RESPONSE_ROWS,), 1, MAX_LENGTH, jnp.int32)
    finished = jax.random.randint(jax.random.fold_in(key, 1), (), 0, RESPONSE_ROWS, jnp.int32)
    return jnp.where(jnp.arange(RESPONSE_ROWS, dtype=jnp.int32) == finished, MAX_LENGTH, base_lengths).astype(jnp.int32)


def draw_block_plan(key, part):
    key = jax.random.fold_in(key, 41)
    shuffled = jax.random.permutation(key, NBLK).astype(jnp.int32)
    return (shuffled % (NBLK // BPD)).astype(jnp.int32)


def level_of(rng, dims, pieces, low, largest):
    gain = 1.0
    for dim, blocks in pieces:
        steps = jax.random.uniform(jax.random.fold_in(jax.random.fold_in(rng, 6), dim), (blocks,), jnp.float32, low / len(pieces), largest / len(pieces))
        gain = gain * jnp.repeat(jnp.exp(steps), dims[dim] // blocks).reshape((-1,) + (1,) * (len(dims) - 1 - dim))
    return gain


def normal_values(stream_key, dims, deviation, bound, pieces=(), kind=jnp.bfloat16):
    drawn = deviation * jax.random.normal(stream_key, dims, jnp.float32)
    if pieces:
        drawn = drawn * level_of(stream_key, dims, pieces, -0.22, 0.18)
    return jnp.clip(drawn, -bound, bound).astype(kind)


def setup_inputs(seed: int = 0) -> dict:
    arg_keys = jax.random.split(jax.random.key(seed), 9)
    key_value_cache = normal_values(arg_keys[0], (GROUP_COUNT, RESPONSE_ROWS, MAX_LENGTH, 2 * KEY_VALUE_HEADS * HEAD_SIZE), 1.0, 6.0, ((0, 2), (1, 16), (3, 8)))
    new_kv = draw_new_kv(jax.random.fold_in(arg_keys[8], 71), 0)
    final_query = draw_final_query(jax.random.fold_in(arg_keys[8], 71), 0)
    out_weight = normal_values(arg_keys[3], (GROUP_COUNT, QUERY_HEADS * HEAD_SIZE, DW), (QUERY_HEADS * HEAD_SIZE // 16) ** -0.5, 0.25, ((0, 2), (1, 8)))
    lengths = draw_lengths(jax.random.fold_in(arg_keys[8], 71), 0)
    block_plan = draw_block_plan(jax.random.fold_in(arg_keys[8], 71), 0)
    queries = draw_queries(jax.random.fold_in(arg_keys[8], 71), 0)
    output_gradient = normal_values(arg_keys[7], (GROUP_COUNT, MAX_LENGTH, QUERY_HEADS * HEAD_SIZE), 1.0, 6.0, ((0, 2), (1, 16), (2, 8)))
    return dict(key_value_cache=key_value_cache, new_kv=new_kv, final_query=final_query, out_weight=out_weight, lengths=lengths, block_plan=block_plan, queries=queries, output_gradient=output_gradient)


neg_big = -1.0e30


def rounded(values):
    return lax.optimization_barrier(values.astype(jnp.bfloat16)).astype(jnp.float32)


def decode_one(operands):
    cached, new_pair, final_query, row_length = operands
    positions = jnp.arange(MAX_LENGTH, dtype=jnp.int32)
    filled_cache = jnp.where((positions == row_length - 1)[:, None], new_pair[None, :], cached)
    reshaped_rows = filled_cache.reshape(MAX_LENGTH, KEY_VALUE_HEADS, 2, HEAD_SIZE).astype(jnp.float32)
    query_matrix = final_query.reshape(KEY_VALUE_HEADS, QUERY_HEADS // KEY_VALUE_HEADS, HEAD_SIZE).astype(jnp.float32)
    scores = jnp.einsum("kgd,lkd->kgl", query_matrix, reshaped_rows[:, :, 0, :]) * HEAD_SIZE ** -0.5
    valid_keys = (positions < row_length)[None, None, :]
    scores = jnp.where(valid_keys, scores, neg_big)
    weights = jnp.where(valid_keys, jnp.exp(scores - jnp.max(scores, axis=-1, keepdims=True)), 0.0)
    mixed = jnp.einsum("kgl,lkd->kgd", rounded(weights), reshaped_rows[:, :, 1, :])
    attended = (mixed / jnp.sum(weights, axis=-1)[..., None]).astype(jnp.bfloat16)
    return attended.reshape(QUERY_HEADS * HEAD_SIZE)


def reference(key_value_cache, new_kv, final_query, out_weight, lengths, block_plan, queries, output_gradient):
    attended = lax.map(decode_one, (key_value_cache[0], new_kv[0], final_query[0], lengths))
    decoded = jnp.dot(attended, out_weight[0], preferred_element_type=jnp.float32).astype(jnp.bfloat16)
    row_ids = jnp.arange(RESPONSE_ROWS, dtype=jnp.int32)
    finished = jnp.sum(jnp.where(lengths == MAX_LENGTH, row_ids, 0)).astype(jnp.int32)
    positions = jnp.arange(MAX_LENGTH, dtype=jnp.int32)
    response_flow = jnp.where((positions == MAX_LENGTH - 1)[:, None], new_kv[0][finished][None, :], key_value_cache[0][finished])
    block_order = jnp.argsort(block_plan, stable=True).astype(jnp.int32)
    planned_rows = (block_order[:, None] * BLK + jnp.arange(BLK, dtype=jnp.int32)[None, :]).reshape(MAX_LENGTH)
    plan_result = response_flow[planned_rows].reshape(MAX_LENGTH, KEY_VALUE_HEADS, 2, HEAD_SIZE).astype(jnp.float32)
    allowed = planned_rows[None, :] <= planned_rows[:, None]
    group_width = QUERY_HEADS // KEY_VALUE_HEADS
    query_layout = queries[1].reshape(MAX_LENGTH, KEY_VALUE_HEADS, group_width, HEAD_SIZE).astype(jnp.float32)
    gradient_grid = output_gradient[1].reshape(MAX_LENGTH, KEY_VALUE_HEADS, group_width, HEAD_SIZE).astype(jnp.float32)
    softmax_scale = HEAD_SIZE ** -0.5

    def one_head(operands):
        key_rows, value_rows, query_matrix, grad_rows = operands
        key_mask = allowed[:, None, :]
        scores = jnp.einsum("igd,jd->igj", query_matrix, key_rows) * softmax_scale
        scores = jnp.where(key_mask, scores, neg_big)
        row_max = jnp.max(scores, axis=-1, keepdims=True)
        weights = jnp.where(key_mask, jnp.exp(scores - row_max), 0.0)
        row_sum = jnp.sum(weights, axis=-1, keepdims=True)
        attention = (jnp.einsum("igj,jd->igd", rounded(weights), value_rows) / row_sum).astype(jnp.bfloat16)
        delta_sum = jnp.sum(grad_rows * lax.optimization_barrier(attention).astype(jnp.float32), axis=-1, keepdims=True)
        row_probs = weights / row_sum
        grad_value = jnp.einsum("igj,igd->jd", rounded(row_probs), grad_rows)
        grad_prob = jnp.einsum("igd,jd->igj", grad_rows, value_rows)
        dscore = rounded(row_probs * (grad_prob - delta_sum))
        query_grad = (jnp.einsum("igj,jd->igd", dscore, key_rows) * softmax_scale).astype(jnp.bfloat16)
        grad_key = jnp.einsum("igj,igd->jd", dscore, query_matrix) * softmax_scale
        return attention, query_grad, jnp.stack([grad_key, grad_value], axis=1)

    attention, query_grad, pair_gradients = lax.map(
        one_head,
        (plan_result[:, :, 0, :].transpose(1, 0, 2), plan_result[:, :, 1, :].transpose(1, 0, 2),
         query_layout.transpose(1, 0, 2, 3), gradient_grid.transpose(1, 0, 2, 3)))
    attention = attention.transpose(1, 0, 2, 3).reshape(MAX_LENGTH, QUERY_HEADS * HEAD_SIZE)
    query_grad = query_grad.transpose(1, 0, 2, 3).reshape(MAX_LENGTH, QUERY_HEADS * HEAD_SIZE)
    pair_gradients = pair_gradients.transpose(1, 0, 2, 3).reshape(MAX_LENGTH, 2 * KEY_VALUE_HEADS * HEAD_SIZE).astype(jnp.bfloat16)
    decoded_all = jnp.stack([decoded, jnp.zeros_like(decoded)])
    attn_all = jnp.stack([jnp.zeros_like(attention), attention])
    query_all = jnp.stack([jnp.zeros_like(query_grad), query_grad])
    pair_all = jnp.stack([jnp.zeros_like(pair_gradients), pair_gradients])
    return (decoded_all, attn_all, query_all, pair_all)
```

```python
import functools
import math

import jax
import jax.numpy as jnp
from jax import lax
from jax.experimental import pallas as pl
from jax.experimental.pallas import tpu as pltpu
from jax.sharding import PartitionSpec as P

HEAD = 128
TOKENS = 64
KEYS = 512
neg_big = -1e30


def attention_kernel(heads, blk, order_ref, meta_ref, *refs):
    pieces, refs = refs[:10], refs[10:]
    q_ref, do_ref, o_ref, dq_ref, g_ref, kv_ref, kt_s, vt_s, s_s, p_s, dk_s, dv_s = refs
    total = kv_ref.shape[0]
    toks = q_ref.shape[0]
    gt, kc = TOKENS, KEYS
    rows = gt * heads
    sub = gt // blk
    me = meta_ref[0]
    learner = meta_ref[1]
    scale = HEAD ** -0.5
    factor = scale * math.log2(math.e)

    @pl.when(learner == 0)
    def _():
        o_ref[...] = jnp.zeros_like(o_ref)
        dq_ref[...] = jnp.zeros_like(dq_ref)
        g_ref[...] = jnp.zeros_like(g_ref)

    @pl.when(learner == 1)
    def _():
        pair = pieces[2].shape[0]
        half = pair // 2
        ring = total // pair
        zi = lax.div(me, 2)
        hi = lax.rem(me, 2)

        def place(ref, back, offset):
            start = lax.rem(zi - back + ring, ring) * pair + offset
            kv_ref[pl.ds(pl.multiple_of(start, half), half), :] = ref

        place(pieces[0][...], 0, hi * half)
        place(pieces[1][...], 0, (1 - hi) * half)
        for i, back in enumerate((1, 2, 3, 7, 6, 5)):
            place(pieces[2 + i][:half], back, 0)
            place(pieces[2 + i][half:], back, half)
        place(pieces[8][...], 4, 0)
        place(pieces[9][...], 4, half)

        for c in range(total // 256):
            part = pl.ds(c * 256, 256)
            kt_s[:, part] = kv_ref[part, :HEAD].T
            vt_s[:, part] = kv_ref[part, HEAD:].T
        dk_s[...] = jnp.zeros_like(dk_s)
        dv_s[...] = jnp.zeros_like(dv_s)

        def stacked(ref, base):
            return jnp.concatenate([ref[pl.ds(base, gt), h * HEAD:(h + 1) * HEAD] for h in range(heads)], axis=0)

        def spread(ref, base, value):
            for h in range(heads):
                ref[pl.ds(base, gt), h * HEAD:(h + 1) * HEAD] = value[h * gt:(h + 1) * gt]

        def group(g, _):
            base = pl.multiple_of(g * gt, gt)
            firsts = [order_ref[me * (toks // blk) + g * sub + s] * blk for s in range(sub)]
            lane = lax.rem(lax.broadcasted_iota(jnp.int32, (1, rows), 1), gt)
            pos = firsts[0] + lane
            for s in range(1, sub):
                pos = jnp.where(lane >= s * blk, firsts[s] + lane - s * blk, pos)
            full = lax.div(firsts[0] + 1, kc)
            last = lax.div(firsts[-1] + blk + kc - 1, kc)
            q = stacked(q_ref, base)
            qt = q.T
            dot_t = stacked(do_ref, base).T

            def scores(masked, c, m):
                part = pl.ds(pl.multiple_of(c * kc, kc), kc)
                s = jnp.dot(kv_ref[part, :HEAD], qt, preferred_element_type=jnp.float32)
                if masked:
                    kpos = c * kc + lax.broadcasted_iota(jnp.int32, (kc, rows), 0)
                    s = jnp.where(kpos <= pos, s, neg_big)
                s_s[part, :] = s
                return jnp.maximum(m, jnp.max(s.reshape(kc // 8, 8, rows), axis=0))

            m = jnp.full((8, rows), neg_big, jnp.float32)
            m = lax.fori_loop(0, full, functools.partial(scores, False), m)
            m = lax.fori_loop(full, last, functools.partial(scores, True), m)
            m = jnp.max(m, axis=0, keepdims=True)

            def weigh(c, carry):
                l, acc = carry
                part = pl.ds(pl.multiple_of(c * kc, kc), kc)
                p = jnp.exp2((s_s[part, :] - m) * factor)
                l = l + jnp.sum(p.reshape(kc // 8, 8, rows), axis=0)
                pb = p.astype(jnp.bfloat16)
                p_s[part, :] = pb
                acc = acc + jnp.dot(vt_s[:, part], pb, preferred_element_type=jnp.float32)
                return l, acc

            l, acc = lax.fori_loop(
                0, last, weigh, (jnp.zeros((8, rows), jnp.float32), jnp.zeros((HEAD, rows), jnp.float32))
            )
            inv = 1.0 / jnp.sum(l, axis=0, keepdims=True)
            ob = (acc * inv).astype(jnp.bfloat16)
            spread(o_ref, base, ob.T)
            dot_f = dot_t.astype(jnp.float32)
            delta = jnp.sum(dot_f * ob.astype(jnp.float32), axis=0, keepdims=True) * inv
            dots = (dot_f * inv).astype(jnp.bfloat16)
            dos = dots.T

            def back(c, acc):
                part = pl.ds(pl.multiple_of(c * kc, kc), kc)
                dp = jnp.dot(kv_ref[part, HEAD:], dots, preferred_element_type=jnp.float32)
                pb = p_s[part, :]
                ds = (pb.astype(jnp.float32) * (dp - delta)).astype(jnp.bfloat16)
                dv_s[part, :] += jnp.dot(pb, dos, preferred_element_type=jnp.float32)
                dk_s[part, :] += jnp.dot(ds, q, preferred_element_type=jnp.float32)
                return acc + jnp.dot(kt_s[:, part], ds, preferred_element_type=jnp.float32)

            acc = lax.fori_loop(0, last, back, jnp.zeros((HEAD, rows), jnp.float32))
            spread(dq_ref, base, (acc * scale).astype(jnp.bfloat16).T)
            return 0

        lax.fori_loop(0, toks // gt, group, 0)

        def put(i, _):
            src = pl.ds(pl.multiple_of(order_ref[i] * blk, blk), blk)
            dst = pl.ds(pl.multiple_of(i * blk, blk), blk)
            g_ref[dst, :HEAD] = (dk_s[src, :] * scale).astype(jnp.bfloat16)
            g_ref[dst, HEAD:] = dv_s[src, :].astype(jnp.bfloat16)
            return 0

        lax.fori_loop(0, total // blk, put, 0)


def attention(order, meta, pieces, q, do, total):
    heads = q.shape[1] // HEAD
    rows = TOKENS * heads
    vmem = pl.BlockSpec(memory_space=pltpu.VMEM)
    smem = pl.BlockSpec(memory_space=pltpu.SMEM)
    rows_like = jax.ShapeDtypeStruct(q.shape, jnp.bfloat16)
    return pl.pallas_call(
        functools.partial(attention_kernel, heads, total // order.shape[0]),
        out_shape=(rows_like, rows_like, jax.ShapeDtypeStruct((total, 2 * HEAD), jnp.bfloat16)),
        in_specs=[smem, smem] + [vmem] * 12,
        out_specs=(vmem, vmem, vmem),
        scratch_shapes=[
            pltpu.VMEM((total, 2 * HEAD), jnp.bfloat16),
            pltpu.VMEM((HEAD, total), jnp.bfloat16),
            pltpu.VMEM((HEAD, total), jnp.bfloat16),
            pltpu.VMEM((total, rows), jnp.float32),
            pltpu.VMEM((total, rows), jnp.bfloat16),
            pltpu.VMEM((total, HEAD), jnp.float32),
            pltpu.VMEM((total, HEAD), jnp.float32),
        ],
        compiler_params=pltpu.CompilerParams(vmem_limit_bytes=48 * 2**20),
    )(order, meta, *pieces, q, do)


def decode_rows(operands):
    cached, new_pair, final_query, row_lengths, weight_rows = operands
    row_count, total, _ = cached.shape
    heads = final_query.shape[1] // HEAD
    positions = jnp.arange(total, dtype=jnp.int32)
    is_last = (positions[None, :] == (row_lengths - 1)[:, None])[:, None, :]
    query = final_query.reshape(row_count, heads, HEAD)
    scores = jnp.einsum("rgd,rld->rgl", query, cached[:, :, :HEAD], preferred_element_type=jnp.float32)
    new_score = jnp.einsum("rgd,rd->rg", query, new_pair[:, :HEAD], preferred_element_type=jnp.float32)
    scores = jnp.where(is_last, new_score[:, :, None], scores) * HEAD ** -0.5
    valid = (positions[None, :] < row_lengths[:, None])[:, None, :]
    scores = jnp.where(valid, scores, neg_big)
    weights = jnp.where(valid, jnp.exp(scores - jnp.max(scores, axis=-1, keepdims=True)), 0.0)
    rounded = weights.astype(jnp.bfloat16)
    old = jnp.where(is_last, jnp.zeros_like(rounded), rounded)
    new = jnp.sum(jnp.where(is_last, rounded.astype(jnp.float32), 0.0), axis=-1)
    mixed = jnp.einsum("rgl,rld->rgd", old, cached[:, :, HEAD:], preferred_element_type=jnp.float32)
    mixed = mixed + new[:, :, None] * new_pair[:, None, HEAD:].astype(jnp.float32)
    attended = (mixed / jnp.sum(weights, axis=-1)[..., None]).astype(jnp.bfloat16)
    return jnp.dot(attended.reshape(row_count, heads * HEAD), weight_rows, preferred_element_type=jnp.float32)


def shards(
    key_value_cache, new_kv, final_query, out_weight, lengths, block_plan, queries, output_gradient
):
    grp_index = lax.axis_index("grp")
    ctx_index = lax.axis_index("ctx")
    ctx_size = lax.axis_size("ctx")
    tp_size = lax.axis_size("tp")
    ring = ctx_size // 2
    cached = key_value_cache[0]
    row_count, total, width = cached.shape
    piece = total // ctx_size
    row_ids = jnp.arange(lengths.shape[0], dtype=jnp.int32)
    finished = jnp.sum(jnp.where(lengths == total, row_ids, 0))
    candidate = lax.dynamic_index_in_dim(cached, finished % row_count, 0, keepdims=False)
    last_pair = lax.dynamic_index_in_dim(new_kv[0], finished % row_count, 0, keepdims=False)

    def scatter_from(root):
        def scatter(operands):
            row, last = operands
            got = jnp.zeros((piece, width), row.dtype)
            for i in range(ctx_size):
                part = row[i * piece:(i + 1) * piece]
                if i == ctx_size - 1:
                    part = part.at[-1].set(last)
                arrived = lax.ppermute(part, ("grp", "ctx"), [(root, ctx_size + i)])
                got = jnp.where(ctx_index == i, arrived, got)
            return got

        return scatter

    mine = lax.switch(
        finished // row_count, [scatter_from(root) for root in range(ctx_size)], (candidate, last_pair)
    )

    def between_learners(x, route):
        return lax.ppermute(x, ("grp", "ctx"), [(ctx_size + i, ctx_size + route(i)) for i in range(ctx_size)])

    def turned(x, step):
        return between_learners(x, lambda i: ((i // 2 + step) % ring) * 2 + i % 2)

    other = between_learners(mine, lambda i: i ^ 1)
    low = ctx_index % 2 == 0
    pair = jnp.concatenate([jnp.where(low, mine, other), jnp.where(low, other, mine)], axis=0)
    right, left = pair, pair
    rights, lefts = [], []
    for _ in range(3):
        right, left = turned(right, 1), turned(left, -1)
        rights.append(right)
        lefts.append(left)
    across = [turned(right[:piece], 1), turned(left[piece:], -1)]
    pieces = [mine, other] + rights + lefts + across

    block_count = block_plan.shape[0]
    order = jnp.argsort(block_plan, stable=True).astype(jnp.int32)
    meta = jnp.stack([ctx_index, grp_index]).astype(jnp.int32)
    attn_out, grad_query, grads = attention(
        order, meta, pieces, queries[0], output_gradient[0], total
    )
    spread = lax.all_to_all(grads.reshape(ctx_size, piece, width), "ctx", 0, 0)
    grad_pairs = jnp.sum(spread.astype(jnp.float32), axis=0).astype(jnp.bfloat16)

    row_lengths = lax.dynamic_slice_in_dim(lengths, ctx_index * row_count, row_count)
    held_query, _ = lax.optimization_barrier((final_query[0], mine))
    partial_out = lax.cond(
        grp_index == 0,
        decode_rows,
        lambda operands: jnp.zeros((row_count, out_weight.shape[2]), jnp.float32),
        (cached, new_kv[0], held_query, row_lengths, out_weight[0]),
    )
    step = 1
    while step < tp_size:
        partial_out = partial_out + lax.ppermute(
            partial_out, ("grp", "tp"), [(i, i ^ step) for i in range(tp_size)]
        )
        step *= 2
    decoded = partial_out.astype(jnp.bfloat16)
    return (decoded[None], attn_out[None], grad_query[None], grad_pairs[None])


def solution(mesh):
    return jax.shard_map(
        shards,
        mesh=mesh,
        in_specs=(
            P("grp", "ctx", None, "tp"),
            P("grp", "ctx", "tp"),
            P("grp", "ctx", "tp"),
            P("grp", "tp", None),
            P(),
            P(),
            P("grp", "ctx", "tp"),
            P("grp", "ctx", "tp"),
        ),
        out_specs=(
            P("grp", "ctx", None),
            P("grp", "ctx", "tp"),
            P("grp", "ctx", "tp"),
            P("grp", "ctx", "tp"),
        ),
        check_vma=False,
    )
```

```python
import functools
import math

import jax
import jax.numpy as jnp
from jax import lax
from jax.experimental import pallas as pl
from jax.experimental.pallas import tpu as pltpu
from jax.sharding import PartitionSpec as P

HEAD = 128
TOKENS = 64
KEYS = 512
neg_big = -1e30


def attention_kernel(heads, blk, order_ref, meta_ref, *refs):
    kv_ref, q_ref, do_ref, o_ref, dq_ref, g_ref, kt_s, vt_s, s_s, p_s, dk_s, dv_s = refs
    total = kv_ref.shape[0]
    toks = q_ref.shape[0]
    gt, kc = TOKENS, KEYS
    rows = gt * heads
    sub = gt // blk
    me = meta_ref[0]
    learner = meta_ref[1]
    scale = HEAD ** -0.5
    factor = scale * math.log2(math.e)

    @pl.when(learner == 0)
    def _():
        o_ref[...] = jnp.zeros_like(o_ref)
        dq_ref[...] = jnp.zeros_like(dq_ref)
        g_ref[...] = jnp.zeros_like(g_ref)

    @pl.when(learner == 1)
    def _():
        for c in range(total // 256):
            part = pl.ds(c * 256, 256)
            kt_s[:, part] = kv_ref[part, :HEAD].T
            vt_s[:, part] = kv_ref[part, HEAD:].T
        dk_s[...] = jnp.zeros_like(dk_s)
        dv_s[...] = jnp.zeros_like(dv_s)

        def stacked(ref, base):
            return jnp.concatenate([ref[pl.ds(base, gt), h * HEAD:(h + 1) * HEAD] for h in range(heads)], axis=0)

        def spread(ref, base, value):
            for h in range(heads):
                ref[pl.ds(base, gt), h * HEAD:(h + 1) * HEAD] = value[h * gt:(h + 1) * gt]

        def group(g, _):
            base = pl.multiple_of(g * gt, gt)
            firsts = [order_ref[me * (toks // blk) + g * sub + s] * blk for s in range(sub)]
            lane = lax.rem(lax.broadcasted_iota(jnp.int32, (1, rows), 1), gt)
            pos = firsts[0] + lane
            for s in range(1, sub):
                pos = jnp.where(lane >= s * blk, firsts[s] + lane - s * blk, pos)
            full = lax.div(firsts[0] + 1, kc)
            last = lax.div(firsts[-1] + blk + kc - 1, kc)
            q = stacked(q_ref, base)
            qt = q.T
            dot_t = stacked(do_ref, base).T

            def scores(masked, c, m):
                part = pl.ds(pl.multiple_of(c * kc, kc), kc)
                s = jnp.dot(kv_ref[part, :HEAD], qt, preferred_element_type=jnp.float32)
                if masked:
                    kpos = c * kc + lax.broadcasted_iota(jnp.int32, (kc, rows), 0)
                    s = jnp.where(kpos <= pos, s, neg_big)
                s_s[part, :] = s
                return jnp.maximum(m, jnp.max(s.reshape(kc // 8, 8, rows), axis=0))

            m = jnp.full((8, rows), neg_big, jnp.float32)
            m = lax.fori_loop(0, full, functools.partial(scores, False), m)
            m = lax.fori_loop(full, last, functools.partial(scores, True), m)
            m = jnp.max(m, axis=0, keepdims=True)

            def weigh(c, carry):
                l, acc = carry
                part = pl.ds(pl.multiple_of(c * kc, kc), kc)
                p = jnp.exp2((s_s[part, :] - m) * factor)
                l = l + jnp.sum(p.reshape(kc // 8, 8, rows), axis=0)
                pb = p.astype(jnp.bfloat16)
                p_s[part, :] = pb
                acc = acc + jnp.dot(vt_s[:, part], pb, preferred_element_type=jnp.float32)
                return l, acc

            l, acc = lax.fori_loop(
                0, last, weigh, (jnp.zeros((8, rows), jnp.float32), jnp.zeros((HEAD, rows), jnp.float32))
            )
            inv = 1.0 / jnp.sum(l, axis=0, keepdims=True)
            ob = (acc * inv).astype(jnp.bfloat16)
            spread(o_ref, base, ob.T)
            dot_f = dot_t.astype(jnp.float32)
            delta = jnp.sum(dot_f * ob.astype(jnp.float32), axis=0, keepdims=True) * inv
            dots = (dot_f * inv).astype(jnp.bfloat16)
            dos = dots.T

            def back(c, acc):
                part = pl.ds(pl.multiple_of(c * kc, kc), kc)
                dp = jnp.dot(kv_ref[part, HEAD:], dots, preferred_element_type=jnp.float32)
                pb = p_s[part, :]
                ds = (pb.astype(jnp.float32) * (dp - delta)).astype(jnp.bfloat16)
                dv_s[part, :] += jnp.dot(pb, dos, preferred_element_type=jnp.float32)
                dk_s[part, :] += jnp.dot(ds, q, preferred_element_type=jnp.float32)
                return acc + jnp.dot(kt_s[:, part], ds, preferred_element_type=jnp.float32)

            acc = lax.fori_loop(0, last, back, jnp.zeros((HEAD, rows), jnp.float32))
            spread(dq_ref, base, (acc * scale).astype(jnp.bfloat16).T)
            return 0

        lax.fori_loop(0, toks // gt, group, 0)

        def put(i, _):
            src = pl.ds(pl.multiple_of(order_ref[i] * blk, blk), blk)
            dst = pl.ds(pl.multiple_of(i * blk, blk), blk)
            g_ref[dst, :HEAD] = (dk_s[src, :] * scale).astype(jnp.bfloat16)
            g_ref[dst, HEAD:] = dv_s[src, :].astype(jnp.bfloat16)
            return 0

        lax.fori_loop(0, total // blk, put, 0)


def attention(order, meta, kv, q, do):
    total = kv.shape[0]
    heads = q.shape[1] // HEAD
    rows = TOKENS * heads
    vmem = pl.BlockSpec(memory_space=pltpu.VMEM)
    smem = pl.BlockSpec(memory_space=pltpu.SMEM)
    rows_like = jax.ShapeDtypeStruct(q.shape, jnp.bfloat16)
    return pl.pallas_call(
        functools.partial(attention_kernel, heads, total // order.shape[0]),
        out_shape=(rows_like, rows_like, jax.ShapeDtypeStruct((total, 2 * HEAD), jnp.bfloat16)),
        in_specs=[smem, smem] + [vmem] * 3,
        out_specs=(vmem, vmem, vmem),
        scratch_shapes=[
            pltpu.VMEM((HEAD, total), jnp.bfloat16),
            pltpu.VMEM((HEAD, total), jnp.bfloat16),
            pltpu.VMEM((total, rows), jnp.float32),
            pltpu.VMEM((total, rows), jnp.bfloat16),
            pltpu.VMEM((total, HEAD), jnp.float32),
            pltpu.VMEM((total, HEAD), jnp.float32),
        ],
        compiler_params=pltpu.CompilerParams(vmem_limit_bytes=48 * 2**20),
    )(order, meta, kv, q, do)


def decode_rows(operands):
    cached, new_pair, final_query, row_lengths, weight_rows = operands
    row_count, total, _ = cached.shape
    heads = final_query.shape[1] // HEAD
    positions = jnp.arange(total, dtype=jnp.int32)
    is_last = (positions[None, :] == (row_lengths - 1)[:, None])[:, None, :]
    query = final_query.reshape(row_count, heads, HEAD)
    scores = jnp.einsum("rgd,rld->rgl", query, cached[:, :, :HEAD], preferred_element_type=jnp.float32)
    new_score = jnp.einsum("rgd,rd->rg", query, new_pair[:, :HEAD], preferred_element_type=jnp.float32)
    scores = jnp.where(is_last, new_score[:, :, None], scores) * HEAD ** -0.5
    valid = (positions[None, :] < row_lengths[:, None])[:, None, :]
    scores = jnp.where(valid, scores, neg_big)
    weights = jnp.where(valid, jnp.exp(scores - jnp.max(scores, axis=-1, keepdims=True)), 0.0)
    rounded = weights.astype(jnp.bfloat16)
    old = jnp.where(is_last, jnp.zeros_like(rounded), rounded)
    new = jnp.sum(jnp.where(is_last, rounded.astype(jnp.float32), 0.0), axis=-1)
    mixed = jnp.einsum("rgl,rld->rgd", old, cached[:, :, HEAD:], preferred_element_type=jnp.float32)
    mixed = mixed + new[:, :, None] * new_pair[:, None, HEAD:].astype(jnp.float32)
    attended = (mixed / jnp.sum(weights, axis=-1)[..., None]).astype(jnp.bfloat16)
    return jnp.dot(attended.reshape(row_count, heads * HEAD), weight_rows, preferred_element_type=jnp.float32)


def shards(
    key_value_cache, new_kv, final_query, out_weight, lengths, block_plan, queries, output_gradient
):
    grp_index = lax.axis_index("grp")
    ctx_index = lax.axis_index("ctx")
    ctx_size = lax.axis_size("ctx")
    tp_size = lax.axis_size("tp")
    ring = ctx_size // 2
    z_index = ctx_index // 2
    cached = key_value_cache[0]
    row_count, total, width = cached.shape
    run = total // ring
    row_ids = jnp.arange(lengths.shape[0], dtype=jnp.int32)
    finished = jnp.sum(jnp.where(lengths == total, row_ids, 0))
    owner = finished // row_count
    owner_z = owner // 2
    picked = finished % row_count
    new_row = lax.dynamic_index_in_dim(new_kv[0], picked, 0, keepdims=True)

    def own_run(i):
        part = lax.dynamic_slice(cached, (picked, i * run, 0), (1, run, width))[0]
        at = i * run + jnp.arange(run, dtype=jnp.int32)
        return jnp.where((at == total - 1)[:, None], new_row, part)

    runs = [own_run((z_index + step) % ring) for step in range(ring)]

    def scatter_from(first):
        def scatter(parts):
            got = parts[0]
            for step in range(1, ring):
                route = [
                    (z * 2 + column, (z + step) % ring * 2 + column)
                    for z in range(first, ring, classes)
                    for column in range(2)
                ]
                arrived = lax.ppermute(parts[step], ("grp", "ctx"), route)
                got = jnp.where((z_index - owner_z) % ring == step, arrived, got)
            return got

        return scatter

    classes = ring // 2
    held = lax.switch(owner_z % classes, [scatter_from(first) for first in range(classes)], runs)

    same = [(i, ctx_size + i) for i in range(ctx_size)]
    flipped = [(i, ctx_size + (i ^ 1)) for i in range(ctx_size)]
    from_same = lax.ppermute(held, ("grp", "ctx"), same)
    from_flipped = lax.ppermute(held, ("grp", "ctx"), flipped)
    mine = jnp.where(owner % 2 == ctx_index % 2, from_same, from_flipped)
    columns = [list(range(column, ctx_size, 2)) for column in range(2)]
    kv = lax.all_gather(mine, "ctx", axis=0, tiled=True, axis_index_groups=columns)

    block_count = block_plan.shape[0]
    order = jnp.argsort(block_plan, stable=True).astype(jnp.int32)
    meta = jnp.stack([ctx_index, grp_index]).astype(jnp.int32)
    attn_out, grad_query, grads = attention(
        order, meta, kv, queries[0], output_gradient[0]
    )
    piece = total // ctx_size
    spread = lax.all_to_all(grads.reshape(ctx_size, piece, width), "ctx", 0, 0)
    grad_pairs = jnp.sum(spread.astype(jnp.float32), axis=0).astype(jnp.bfloat16)

    row_lengths = lax.dynamic_slice_in_dim(lengths, ctx_index * row_count, row_count)
    held_query, _ = lax.optimization_barrier((final_query[0], held))
    partial_out = lax.cond(
        grp_index == 0,
        decode_rows,
        lambda operands: jnp.zeros((row_count, out_weight.shape[2]), jnp.float32),
        (cached, new_kv[0], held_query, row_lengths, out_weight[0]),
    )
    step = 1
    while step < tp_size:
        partial_out = partial_out + lax.ppermute(
            partial_out, ("grp", "tp"), [(i, i ^ step) for i in range(tp_size)]
        )
        step *= 2
    decoded = partial_out.astype(jnp.bfloat16)
    return (decoded[None], attn_out[None], grad_query[None], grad_pairs[None])


def solution(mesh):
    return jax.shard_map(
        shards,
        mesh=mesh,
        in_specs=(
            P("grp", "ctx", None, "tp"),
            P("grp", "ctx", "tp"),
            P("grp", "ctx", "tp"),
            P("grp", "tp", None),
            P(),
            P(),
            P("grp", "ctx", "tp"),
            P("grp", "ctx", "tp"),
        ),
        out_specs=(
            P("grp", "ctx", None),
            P("grp", "ctx", "tp"),
            P("grp", "ctx", "tp"),
            P("grp", "ctx", "tp"),
        ),
        check_vma=False,
    )
```

```python
import functools
import itertools
import math

import jax
import jax.numpy as jnp
from jax import lax
from jax.experimental import pallas as pl
from jax.experimental.pallas import tpu as pltpu
from jax.sharding import PartitionSpec as P

HEAD = 128
TOKENS = 64
KEYS = 512
neg_big = -1e30


def attention_kernel(heads, blk, order_ref, meta_ref, *refs):
    pieces, refs = refs[:6], refs[6:]
    in_ref, out_ref, keep_ref, send_ref, kv_ref, kt_s, vt_s, s_s, p_s, dk_s, dv_s = refs
    total = kv_ref.shape[0]
    toks = in_ref.shape[1]
    gt, kc = TOKENS, KEYS
    rows = gt * heads
    sub = gt // blk
    me = meta_ref[0]
    learner = meta_ref[1]
    core = meta_ref[2]
    scale = HEAD ** -0.5
    factor = scale * math.log2(math.e)

    @pl.when(learner == 0)
    def _():
        out_ref[...] = jnp.zeros_like(out_ref)
        keep_ref[...] = jnp.zeros_like(keep_ref)
        send_ref[...] = jnp.zeros_like(send_ref)

    @pl.when(learner == 1)
    def _():
        run = pieces[0].shape[0]
        half = run // 2
        ring = total // run
        z = lax.div(me, 2)
        turn = 1 - 2 * core

        def place(ref, first, size, steps, offset):
            start = lax.rem(z + steps + ring, ring) * run + offset
            for r in range(0, size, half):
                kv_ref[pl.ds(pl.multiple_of(start + r, half), half), :] = ref[pl.ds(first + r, half), :]

        place(pieces[0], 0, run, 0, 0)
        for i in range(3):
            place(pieces[1 + i], 0, run, -turn * (i + 1), 0)
            place(pieces[5], i * run, run, turn * (i + 1), 0)
        place(pieces[4], 0, half, 4, core * half)
        place(pieces[5], 3 * run, half, 4, (1 - core) * half)

        for c in range(total // 256):
            part = pl.ds(c * 256, 256)
            kt_s[:, part] = kv_ref[part, :HEAD].T
            vt_s[:, part] = kv_ref[part, HEAD:].T
        dk_s[...] = jnp.zeros_like(dk_s)
        dv_s[...] = jnp.zeros_like(dv_s)

        def stacked(which, base):
            return jnp.concatenate([in_ref[which, pl.ds(base, gt), h * HEAD:(h + 1) * HEAD] for h in range(heads)], axis=0)

        def spread(which, base, value):
            for h in range(heads):
                out_ref[which, pl.ds(base, gt), h * HEAD:(h + 1) * HEAD] = value[h * gt:(h + 1) * gt]

        def group(g, _):
            base = pl.multiple_of(g * gt, gt)
            firsts = [order_ref[me * (toks // blk) + g * sub + s] * blk for s in range(sub)]
            lane = lax.rem(lax.broadcasted_iota(jnp.int32, (1, rows), 1), gt)
            pos = firsts[0] + lane
            for s in range(1, sub):
                pos = jnp.where(lane >= s * blk, firsts[s] + lane - s * blk, pos)
            full = lax.div(firsts[0] + 1, kc)
            last = lax.div(firsts[-1] + blk + kc - 1, kc)
            q = stacked(0, base)
            qt = q.T
            dot_t = stacked(1, base).T

            def scores(masked, c, m):
                part = pl.ds(pl.multiple_of(c * kc, kc), kc)
                s = jnp.dot(kv_ref[part, :HEAD], qt, preferred_element_type=jnp.float32)
                if masked:
                    kpos = c * kc + lax.broadcasted_iota(jnp.int32, (kc, rows), 0)
                    s = jnp.where(kpos <= pos, s, neg_big)
                s_s[part, :] = s
                return jnp.maximum(m, jnp.max(s.reshape(kc // 8, 8, rows), axis=0))

            m = jnp.full((8, rows), neg_big, jnp.float32)
            m = lax.fori_loop(0, full, functools.partial(scores, False), m)
            m = lax.fori_loop(full, last, functools.partial(scores, True), m)
            m = jnp.max(m, axis=0, keepdims=True)

            def weigh(c, carry):
                l, acc = carry
                part = pl.ds(pl.multiple_of(c * kc, kc), kc)
                p = jnp.exp2((s_s[part, :] - m) * factor)
                l = l + jnp.sum(p.reshape(kc // 8, 8, rows), axis=0)
                pb = p.astype(jnp.bfloat16)
                p_s[part, :] = pb
                acc = acc + jnp.dot(vt_s[:, part], pb, preferred_element_type=jnp.float32)
                return l, acc

            l, acc = lax.fori_loop(
                0, last, weigh, (jnp.zeros((8, rows), jnp.float32), jnp.zeros((HEAD, rows), jnp.float32))
            )
            inv = 1.0 / jnp.sum(l, axis=0, keepdims=True)
            ob = (acc * inv).astype(jnp.bfloat16)
            spread(0, base, ob.T)
            dot_f = dot_t.astype(jnp.float32)
            delta = jnp.sum(dot_f * ob.astype(jnp.float32), axis=0, keepdims=True) * inv
            dots = (dot_f * inv).astype(jnp.bfloat16)
            dos = dots.T

            def back(c, acc):
                part = pl.ds(pl.multiple_of(c * kc, kc), kc)
                dp = jnp.dot(kv_ref[part, HEAD:], dots, preferred_element_type=jnp.float32)
                pb = p_s[part, :]
                ds = (pb.astype(jnp.float32) * (dp - delta)).astype(jnp.bfloat16)
                dv_s[part, :] += jnp.dot(pb, dos, preferred_element_type=jnp.float32)
                dk_s[part, :] += jnp.dot(ds, q, preferred_element_type=jnp.float32)
                return acc + jnp.dot(kt_s[:, part], ds, preferred_element_type=jnp.float32)

            acc = lax.fori_loop(0, last, back, jnp.zeros((HEAD, rows), jnp.float32))
            spread(1, base, (acc * scale).astype(jnp.bfloat16).T)
            return 0

        lax.fori_loop(0, toks // gt, group, 0)

        per = toks // blk

        def put(parity, ref, i, _):
            shard = lax.div(i, per) * 2 + parity
            src = pl.ds(pl.multiple_of(order_ref[shard * per + lax.rem(i, per)] * blk, blk), blk)
            dst = pl.ds(pl.multiple_of(i * blk, blk), blk)
            ref[dst, :HEAD] = (dk_s[src, :] * scale).astype(ref.dtype)
            ref[dst, HEAD:] = dv_s[src, :].astype(ref.dtype)
            return 0

        lax.fori_loop(0, total // blk // 2, functools.partial(put, core, keep_ref), 0)
        lax.fori_loop(0, total // blk // 2, functools.partial(put, 1 - core, send_ref), 0)


def attention(order, meta, pieces, token_rows, total):
    heads = token_rows.shape[2] // HEAD
    rows = TOKENS * heads
    vmem = pl.BlockSpec(memory_space=pltpu.VMEM)
    smem = pl.BlockSpec(memory_space=pltpu.SMEM)
    return pl.pallas_call(
        functools.partial(attention_kernel, heads, total // order.shape[0]),
        out_shape=(
            jax.ShapeDtypeStruct(token_rows.shape, jnp.bfloat16),
            jax.ShapeDtypeStruct((total // 2, 2 * HEAD), jnp.float32),
            jax.ShapeDtypeStruct((total // 2, 2 * HEAD), jnp.bfloat16),
        ),
        in_specs=[smem, smem] + [vmem] * 7,
        out_specs=(vmem, vmem, vmem),
        scratch_shapes=[
            pltpu.VMEM((total, 2 * HEAD), jnp.bfloat16),
            pltpu.VMEM((HEAD, total), jnp.bfloat16),
            pltpu.VMEM((HEAD, total), jnp.bfloat16),
            pltpu.VMEM((total, rows), jnp.float32),
            pltpu.VMEM((total, rows), jnp.bfloat16),
            pltpu.VMEM((total, HEAD), jnp.float32),
            pltpu.VMEM((total, HEAD), jnp.float32),
        ],
        compiler_params=pltpu.CompilerParams(vmem_limit_bytes=48 * 2**20),
    )(order, meta, *pieces, token_rows)


def decode_rows(operands):
    cached, new_pair, final_query, row_lengths, weight_rows = operands
    row_count, total, _ = cached.shape
    heads = final_query.shape[1] // HEAD
    positions = jnp.arange(total, dtype=jnp.int32)
    is_last = (positions[None, :] == (row_lengths - 1)[:, None])[:, None, :]
    query = final_query.reshape(row_count, heads, HEAD)
    scores = jnp.einsum("rgd,rld->rgl", query, cached[:, :, :HEAD], preferred_element_type=jnp.float32)
    new_score = jnp.einsum("rgd,rd->rg", query, new_pair[:, :HEAD], preferred_element_type=jnp.float32)
    scores = jnp.where(is_last, new_score[:, :, None], scores) * HEAD ** -0.5
    valid = (positions[None, :] < row_lengths[:, None])[:, None, :]
    scores = jnp.where(valid, scores, neg_big)
    weights = jnp.where(valid, jnp.exp(scores - jnp.max(scores, axis=-1, keepdims=True)), 0.0)
    rounded = weights.astype(jnp.bfloat16)
    old = jnp.where(is_last, jnp.zeros_like(rounded), rounded)
    new = jnp.sum(jnp.where(is_last, rounded.astype(jnp.float32), 0.0), axis=-1)
    mixed = jnp.einsum("rgl,rld->rgd", old, cached[:, :, HEAD:], preferred_element_type=jnp.float32)
    mixed = mixed + new[:, :, None] * new_pair[:, None, HEAD:].astype(jnp.float32)
    attended = (mixed / jnp.sum(weights, axis=-1)[..., None]).astype(jnp.bfloat16)
    return jnp.dot(attended.reshape(row_count, heads * HEAD), weight_rows, preferred_element_type=jnp.float32)


def shards(
    key_value_cache, new_kv, final_query, out_weight, lengths, block_plan, queries, output_gradient
):
    grp_index = lax.axis_index("grp")
    ctx_index = lax.axis_index("ctx")
    ctx_size = lax.axis_size("ctx")
    tp_size = lax.axis_size("tp")
    ring = ctx_size // 2
    z_index, column = ctx_index >> 1, ctx_index & 1
    core = lax.axis_index("tp") & 1

    def route(groups, move):
        pairs = []
        for at in itertools.product(groups, range(ring), range(2), range(tp_size // 2), range(2)):
            to = move(*at)
            if to is not None and to != at:
                pairs.append(tuple((((g * ring + z) * 2 + h) * tp_size) + y * 2 + c for g, z, h, y, c in (at, to)))
        return pairs

    def sent(x, pairs):
        return lax.ppermute(x, ("grp", "ctx", "tp"), pairs)

    swap = route((1,), lambda g, z, h, y, c: (g, z, c, y, h))
    cores = route((0, 1), lambda g, z, h, y, c: (g, z, h, y, 1 - c))
    around = route((1,), lambda g, z, h, y, c: (g, (z + 1 - 2 * c) % ring, h, y, c))
    across = route((0,), lambda g, z, h, y, c: (1, z, c, y, h))

    stays = column == core
    token_rows = jnp.stack([queries[0], output_gradient[0]])
    token_rows = jnp.where(stays, token_rows, sent(token_rows, swap))
    cached = key_value_cache[0]
    row_count, total, width = cached.shape
    run = total // ring
    row_ids = jnp.arange(lengths.shape[0], dtype=jnp.int32)
    finished = jnp.sum(jnp.where(lengths == total, row_ids, 0))
    owner = lax.div(finished, row_count)
    owner_z = owner >> 1
    picked = lax.rem(finished, row_count)
    distance = lax.rem(z_index + ring - owner_z, ring)
    new_row = lax.dynamic_slice(new_kv[0], (picked, 0), (1, width), allow_negative_indices=False)

    def own_run(i):
        part = lax.dynamic_slice(
            cached, (picked, i * run, 0), (1, run, width), allow_negative_indices=False
        )[0]
        at = i * run + jnp.arange(run, dtype=jnp.int32)
        return jnp.where((at == total - 1)[:, None], new_row, part)

    runs = [own_run(lax.rem(z_index + step, ring)) for step in range(ring)]

    def scatter_from(first):
        def scatter(parts):
            got = parts[0]
            for step in range(1, ring):
                route = [
                    (z * 2 + column, (z + step) % ring * 2 + column)
                    for z in range(first, ring, classes)
                    for column in range(2)
                ]
                arrived = lax.ppermute(parts[step], ("grp", "ctx"), route)
                got = jnp.where(distance == step, arrived, got)
            return got

        return scatter

    classes = ring // 2
    held = lax.switch(lax.rem(owner_z, classes), [scatter_from(first) for first in range(classes)], runs)

    landed = sent(held, across)
    landed, token_rows, order = lax.optimization_barrier(
        (landed, token_rows, jnp.argsort(block_plan, stable=True).astype(jnp.int32))
    )
    own = jnp.where(core == (owner & 1), landed, sent(landed, cores))
    half = run // 2
    passing, arrived = own, []
    for step in range(4):
        if step == 3:
            passing = jnp.where(core == 0, passing[:half], passing[half:])
        passing = sent(passing, around)
        arrived.append(passing)
    other = sent(jnp.concatenate(arrived, axis=0), cores)
    pieces = [own] + arrived + [other]

    meta = jnp.stack([z_index * 2 + core, grp_index, core]).astype(jnp.int32)
    result_rows, kept, passed = attention(order, meta, pieces, token_rows, total)
    summed = (kept + sent(passed, cores).astype(jnp.float32)).astype(jnp.bfloat16)
    columns = [list(range(h, ctx_size, 2)) for h in range(2)]
    spread = lax.all_to_all(
        summed.reshape(ring, total // ctx_size, width), "ctx", 0, 0, axis_index_groups=columns
    )
    grads = jnp.sum(spread.astype(jnp.float32), axis=0).astype(jnp.bfloat16)
    returned = sent(result_rows, swap)
    attn_out = jnp.where(stays, result_rows[0], returned[0])
    grad_query = jnp.where(stays, result_rows[1], returned[1])
    grad_pairs = jnp.where(stays, grads, sent(grads, swap))

    row_lengths = lax.dynamic_slice_in_dim(lengths, ctx_index * row_count, row_count)
    held_query, _ = lax.optimization_barrier((final_query[0], held))
    partial_out = lax.cond(
        grp_index == 0,
        decode_rows,
        lambda operands: jnp.zeros((row_count, out_weight.shape[2]), jnp.float32),
        (cached, new_kv[0], held_query, row_lengths, out_weight[0]),
    )
    partial_out = partial_out + sent(partial_out, cores)
    partial_out = partial_out + sent(partial_out, route((0,), lambda g, z, h, y, c: (g, z, h, y ^ 1, c)))
    partial_out = partial_out + sent(partial_out, route((0,), lambda g, z, h, y, c: (g, z, h, y ^ 2, c)))
    decoded = partial_out.astype(jnp.bfloat16)
    return (decoded[None], attn_out[None], grad_query[None], grad_pairs[None])


def solution(mesh):
    return jax.shard_map(
        shards,
        mesh=mesh,
        in_specs=(
            P("grp", "ctx", None, "tp"),
            P("grp", "ctx", "tp"),
            P("grp", "ctx", "tp"),
            P("grp", "tp", None),
            P(),
            P(),
            P("grp", "ctx", "tp"),
            P("grp", "ctx", "tp"),
        ),
        out_specs=(
            P("grp", "ctx", None),
            P("grp", "ctx", "tp"),
            P("grp", "ctx", "tp"),
            P("grp", "ctx", "tp"),
        ),
        check_vma=False,
    )
```

```python
import functools
import itertools
import math

import jax
import jax.numpy as jnp
from jax import lax
from jax.experimental import pallas as pl
from jax.experimental.pallas import tpu as pltpu
from jax.sharding import PartitionSpec as P

HEAD = 128
TOKENS = 96
KEYS = 768
neg_big = -1e30


def attention_kernel(heads, blk, order_ref, meta_ref, *refs):
    mine_ref, other_ref, q_ref, do_ref, o_ref, dq_ref, keep_ref, send_ref, kv_ref, kt_s, vt_s, s_s, p_s, dk_s, dv_s = refs
    total = kv_ref.shape[0]
    toks = q_ref.shape[0]
    gt, kc = TOKENS, KEYS
    rows = gt * heads
    sub = gt // blk
    me = meta_ref[0]
    learner = meta_ref[1]
    core = meta_ref[2]
    scale = HEAD ** -0.5
    factor = scale * math.log2(math.e)

    @pl.when(learner == 0)
    def _():
        o_ref[...] = jnp.zeros_like(o_ref)
        dq_ref[...] = jnp.zeros_like(dq_ref)
        keep_ref[...] = jnp.zeros_like(keep_ref)
        send_ref[...] = jnp.zeros_like(send_ref)

    @pl.when(learner == 1)
    def _():
        half = toks
        for r in range(total // half // 2):
            for ref, which in ((mine_ref, core), (other_ref, 1 - core)):
                start = pl.multiple_of((2 * r + which) * half, half)
                kv_ref[pl.ds(start, half), :] = ref[r * half:(r + 1) * half, :]

        for c in range(total // 256):
            part = pl.ds(c * 256, 256)
            kt_s[:, part] = kv_ref[part, :HEAD].T
            vt_s[:, part] = kv_ref[part, HEAD:].T
        dk_s[...] = jnp.zeros_like(dk_s)
        dv_s[...] = jnp.zeros_like(dv_s)

        def stacked(ref, base):
            return jnp.concatenate([ref[pl.ds(base, gt), h * HEAD:(h + 1) * HEAD] for h in range(heads)], axis=0)

        def spread(ref, base, value):
            for h in range(heads):
                ref[pl.ds(base, gt), h * HEAD:(h + 1) * HEAD] = value[h * gt:(h + 1) * gt]

        def group(g, _):
            base = pl.multiple_of(g * gt, gt)
            firsts = [order_ref[me * (toks // blk) + g * sub + s] * blk for s in range(sub)]
            lane = lax.rem(lax.broadcasted_iota(jnp.int32, (1, rows), 1), gt)
            pos = firsts[0] + lane
            for s in range(1, sub):
                pos = jnp.where(lane >= s * blk, firsts[s] + lane - s * blk, pos)
            full = lax.div(firsts[0] + 1, kc)
            last = lax.div(firsts[-1] + blk + kc - 1, kc)
            q = stacked(q_ref, base)
            qt = q.T
            dot_t = stacked(do_ref, base).T

            def scores(masked, c, m):
                part = pl.ds(pl.multiple_of(c * kc, kc), kc)
                s = jnp.dot(kv_ref[part, :HEAD], qt, preferred_element_type=jnp.float32)
                if masked:
                    kpos = c * kc + lax.broadcasted_iota(jnp.int32, (kc, rows), 0)
                    s = jnp.where(kpos <= pos, s, neg_big)
                s_s[part, :] = s
                return jnp.maximum(m, jnp.max(s.reshape(kc // 8, 8, rows), axis=0))

            m = jnp.full((8, rows), neg_big, jnp.float32)
            m = lax.fori_loop(0, full, functools.partial(scores, False), m)
            m = lax.fori_loop(full, last, functools.partial(scores, True), m)
            m = jnp.max(m, axis=0, keepdims=True)

            def weigh(c, carry):
                l, acc = carry
                part = pl.ds(pl.multiple_of(c * kc, kc), kc)
                p = jnp.exp2((s_s[part, :] - m) * factor)
                l = l + jnp.sum(p.reshape(kc // 8, 8, rows), axis=0)
                pb = p.astype(jnp.bfloat16)
                p_s[part, :] = pb
                acc = acc + jnp.dot(vt_s[:, part], pb, preferred_element_type=jnp.float32)
                return l, acc

            l, acc = lax.fori_loop(
                0, last, weigh, (jnp.zeros((8, rows), jnp.float32), jnp.zeros((HEAD, rows), jnp.float32))
            )
            inv = 1.0 / jnp.sum(l, axis=0, keepdims=True)
            ob = (acc * inv).astype(jnp.bfloat16)
            spread(o_ref, base, ob.T)
            dot_f = dot_t.astype(jnp.float32)
            delta = jnp.sum(dot_f * ob.astype(jnp.float32), axis=0, keepdims=True) * inv
            dots = (dot_f * inv).astype(jnp.bfloat16)
            dos = dots.T

            def back(c, acc):
                part = pl.ds(pl.multiple_of(c * kc, kc), kc)
                dp = jnp.dot(kv_ref[part, HEAD:], dots, preferred_element_type=jnp.float32)
                pb = p_s[part, :]
                ds = (pb.astype(jnp.float32) * (dp - delta)).astype(jnp.bfloat16)
                dv_s[part, :] += jnp.dot(pb, dos, preferred_element_type=jnp.float32)
                dk_s[part, :] += jnp.dot(ds, q, preferred_element_type=jnp.float32)
                return acc + jnp.dot(kt_s[:, part], ds, preferred_element_type=jnp.float32)

            acc = lax.fori_loop(0, last, back, jnp.zeros((HEAD, rows), jnp.float32))
            spread(dq_ref, base, (acc * scale).astype(jnp.bfloat16).T)
            return 0

        lax.fori_loop(0, toks // gt, group, 0)

        per = toks // blk

        def put(parity, ref, i, _):
            shard = lax.div(i, per) * 2 + parity
            src = pl.ds(pl.multiple_of(order_ref[shard * per + lax.rem(i, per)] * blk, blk), blk)
            dst = pl.ds(pl.multiple_of(i * blk, blk), blk)
            ref[dst, :HEAD] = (dk_s[src, :] * scale).astype(ref.dtype)
            ref[dst, HEAD:] = dv_s[src, :].astype(ref.dtype)
            return 0

        lax.fori_loop(0, total // blk // 2, functools.partial(put, core, keep_ref), 0, unroll=8)
        lax.fori_loop(0, total // blk // 2, functools.partial(put, 1 - core, send_ref), 0, unroll=8)


def attention(order, meta, mine, other, q, do):
    total = mine.shape[0] * 2
    heads = q.shape[1] // HEAD
    rows = TOKENS * heads
    vmem = pl.BlockSpec(memory_space=pltpu.VMEM)
    smem = pl.BlockSpec(memory_space=pltpu.SMEM)
    return pl.pallas_call(
        functools.partial(attention_kernel, heads, total // order.shape[0]),
        out_shape=(
            jax.ShapeDtypeStruct(q.shape, jnp.bfloat16),
            jax.ShapeDtypeStruct(q.shape, jnp.bfloat16),
            jax.ShapeDtypeStruct((total // 2, 2 * HEAD), jnp.float32),
            jax.ShapeDtypeStruct((total // 2, 2 * HEAD), jnp.bfloat16),
        ),
        in_specs=[smem, smem] + [vmem] * 4,
        out_specs=(vmem, vmem, vmem, vmem),
        scratch_shapes=[
            pltpu.VMEM((total, 2 * HEAD), jnp.bfloat16),
            pltpu.VMEM((HEAD, total), jnp.bfloat16),
            pltpu.VMEM((HEAD, total), jnp.bfloat16),
            pltpu.VMEM((total, rows), jnp.float32),
            pltpu.VMEM((total, rows), jnp.bfloat16),
            pltpu.VMEM((total, HEAD), jnp.float32),
            pltpu.VMEM((total, HEAD), jnp.float32),
        ],
        compiler_params=pltpu.CompilerParams(vmem_limit_bytes=48 * 2**20),
    )(order, meta, mine, other, q, do)


def runs_kernel(lengths_ref, z_ref, cached_ref, new_ref, owner_ref, *refs):
    run_refs, sems = refs[:-1], refs[-1]
    ring = len(run_refs)
    run = run_refs[0].shape[0]
    row_count, total, _ = cached_ref.shape
    finished = jnp.int32(0)
    for r in range(lengths_ref.shape[0]):
        finished = jnp.where(lengths_ref[r] == total, r, finished)
    picked = lax.rem(finished, row_count)
    owner_ref[0] = lax.div(finished, row_count)
    copies = []
    for step, ref in enumerate(run_refs):
        start = pl.multiple_of(lax.rem(z_ref[0] + step, ring) * run, run)
        copies.append(pltpu.make_async_copy(cached_ref.at[picked, pl.ds(start, run)], ref, sems.at[step]))
    for copy in copies:
        copy.start()
    new_row = new_ref[0:1, :]
    for r in range(1, row_count):
        new_row = jnp.where(picked == r, new_ref[r:r + 1, :], new_row)
    for copy in copies:
        copy.wait()
    for step, ref in enumerate(run_refs):
        @pl.when(lax.rem(z_ref[0] + step, ring) == ring - 1)
        def _(ref=ref):
            at = lax.broadcasted_iota(jnp.int32, (16, ref.shape[1]), 0)
            tail = pl.ds(run - 16, 16)
            ref[tail, :] = jnp.where(at == 15, new_row, ref[tail, :])


def finished_runs(lengths, z_index, cached, new_pairs, ring):
    total, width = cached.shape[1:]
    vmem = pl.BlockSpec(memory_space=pltpu.VMEM)
    smem = pl.BlockSpec(memory_space=pltpu.SMEM)
    return pl.pallas_call(
        runs_kernel,
        out_shape=[jax.ShapeDtypeStruct((1,), jnp.int32)]
        + [jax.ShapeDtypeStruct((total // ring, width), cached.dtype)] * ring,
        in_specs=[smem, smem, pl.BlockSpec(memory_space=pl.ANY), vmem],
        out_specs=[smem] + [vmem] * ring,
        scratch_shapes=[pltpu.SemaphoreType.DMA((ring,))],
        compiler_params=pltpu.CompilerParams(vmem_limit_bytes=16 * 2**20),
    )(lengths, z_index.reshape(1), cached, new_pairs)


def decode_rows(operands):
    cached, new_pair, final_query, row_lengths, weight_rows = operands
    row_count, total, _ = cached.shape
    heads = final_query.shape[1] // HEAD
    positions = jnp.arange(total, dtype=jnp.int32)
    is_last = (positions[None, :] == (row_lengths - 1)[:, None])[:, None, :]
    query = final_query.reshape(row_count, heads, HEAD)
    scores = jnp.einsum("rgd,rld->rgl", query, cached[:, :, :HEAD], preferred_element_type=jnp.float32)
    new_score = jnp.einsum("rgd,rd->rg", query, new_pair[:, :HEAD], preferred_element_type=jnp.float32)
    scores = jnp.where(is_last, new_score[:, :, None], scores) * HEAD ** -0.5
    valid = (positions[None, :] < row_lengths[:, None])[:, None, :]
    scores = jnp.where(valid, scores, neg_big)
    weights = jnp.where(valid, jnp.exp(scores - jnp.max(scores, axis=-1, keepdims=True)), 0.0)
    rounded = weights.astype(jnp.bfloat16)
    old = jnp.where(is_last, jnp.zeros_like(rounded), rounded)
    new = jnp.sum(jnp.where(is_last, rounded.astype(jnp.float32), 0.0), axis=-1)
    mixed = jnp.einsum("rgl,rld->rgd", old, cached[:, :, HEAD:], preferred_element_type=jnp.float32)
    mixed = mixed + new[:, :, None] * new_pair[:, None, HEAD:].astype(jnp.float32)
    attended = (mixed / jnp.sum(weights, axis=-1)[..., None]).astype(jnp.bfloat16)
    return jnp.dot(attended.reshape(row_count, heads * HEAD), weight_rows, preferred_element_type=jnp.float32)


def shards(
    key_value_cache, new_kv, final_query, out_weight, lengths, block_plan, queries, output_gradient
):
    grp_index = lax.axis_index("grp")
    ctx_index = lax.axis_index("ctx")
    ctx_size = lax.axis_size("ctx")
    tp_size = lax.axis_size("tp")
    ring = ctx_size // 2
    z_index, column = ctx_index >> 1, ctx_index & 1
    core = lax.axis_index("tp") & 1

    def route(groups, move, stay=False):
        pairs = []
        for at in itertools.product(groups, range(ring), range(2), range(tp_size // 2), range(2)):
            to = move(*at)
            if stay or to != at:
                pairs.append(tuple((((g * ring + z) * 2 + h) * tp_size) + y * 2 + c for g, z, h, y, c in (at, to)))
        return pairs

    def sent(x, pairs):
        return lax.ppermute(x, ("grp", "ctx", "tp"), pairs)

    swap = route((1,), lambda g, z, h, y, c: (g, z, c, y, h))
    swap_all = route((1,), lambda g, z, h, y, c: (g, z, c, y, h), True)
    cores = route((0, 1), lambda g, z, h, y, c: (g, z, h, y, 1 - c))
    across = route((0,), lambda g, z, h, y, c: (1, z, c, y, h))

    cached = key_value_cache[0]
    row_count, total, width = cached.shape
    run = total // ring
    half = run // 2
    owner, *runs = finished_runs(lengths, z_index, cached, new_kv[0], ring)
    owner = owner[0]
    owner_z = owner >> 1
    distance = lax.rem(z_index + ring - owner_z, ring)

    def scatter_from(first):
        def scatter(parts):
            got = parts[0]
            for step in range(1, ring):
                route = [
                    (z * 2 + column, (z + step) % ring * 2 + column)
                    for z in range(first, ring, classes)
                    for column in range(2)
                ]
                arrived = lax.ppermute(parts[step], ("grp", "ctx"), route)
                got = jnp.where(distance == step, arrived, got)
            return got

        return scatter

    classes = ring // 2
    held = lax.switch(lax.rem(owner_z, classes), [scatter_from(first) for first in range(classes)], runs)

    stays = column == core
    query_rows = sent(queries[0], swap_all)
    gradient_rows = sent(output_gradient[0], swap)
    gradient_rows = jnp.where(stays, output_gradient[0], gradient_rows)
    landed = sent(held, across)
    landed, query_rows, gradient_rows, order = lax.optimization_barrier(
        (landed, query_rows, gradient_rows, jnp.argsort(block_plan, stable=True).astype(jnp.int32))
    )
    low, high = landed[:half], landed[half:]
    handed = sent(jnp.where(core == 0, high, low), cores)
    own = jnp.where(core == (owner & 1), jnp.where(core == 0, low, high), handed)
    columns = [list(range(h, ctx_size, 2)) for h in range(2)]
    mine = lax.all_gather(own, "ctx", axis=0, tiled=True, axis_index_groups=columns)
    other = sent(mine, cores)

    meta = jnp.stack([z_index * 2 + core, grp_index, core]).astype(jnp.int32)
    attn_rows, grad_rows, kept, passed = attention(order, meta, mine, other, query_rows, gradient_rows)
    summed = (kept + sent(passed, cores).astype(jnp.float32)).astype(jnp.bfloat16)
    spread = lax.all_to_all(
        summed.reshape(ring, total // ctx_size, width), "ctx", 0, 0, axis_index_groups=columns
    )
    attn_out = sent(attn_rows, swap_all)
    grad_query = jnp.where(stays, grad_rows, sent(grad_rows, swap))
    grads = jnp.sum(spread.astype(jnp.float32), axis=0).astype(jnp.bfloat16)
    grad_pairs = sent(grads, swap_all)

    row_lengths = lax.dynamic_slice_in_dim(lengths, ctx_index * row_count, row_count)
    held_query, _ = lax.optimization_barrier((final_query[0], held))
    partial_out = lax.cond(
        grp_index == 0,
        decode_rows,
        lambda operands: jnp.zeros((row_count, out_weight.shape[2]), jnp.float32),
        (cached, new_kv[0], held_query, row_lengths, out_weight[0]),
    )
    partial_out = partial_out + sent(partial_out, cores)
    partial_out = partial_out + sent(partial_out, route((0,), lambda g, z, h, y, c: (g, z, h, y ^ 1, c)))
    partial_out = partial_out + sent(partial_out, route((0,), lambda g, z, h, y, c: (g, z, h, y ^ 2, c)))
    decoded = partial_out.astype(jnp.bfloat16)
    return (decoded[None], attn_out[None], grad_query[None], grad_pairs[None])


def solution(mesh):
    return jax.shard_map(
        shards,
        mesh=mesh,
        in_specs=(
            P("grp", "ctx", None, "tp"),
            P("grp", "ctx", "tp"),
            P("grp", "ctx", "tp"),
            P("grp", "tp", None),
            P(),
            P(),
            P("grp", "ctx", "tp"),
            P("grp", "ctx", "tp"),
        ),
        out_specs=(
            P("grp", "ctx", None),
            P("grp", "ctx", "tp"),
            P("grp", "ctx", "tp"),
            P("grp", "ctx", "tp"),
        ),
        check_vma=False,
    )
```

```python
import functools
import itertools
import math

import jax
import jax.numpy as jnp
from jax import lax
from jax.experimental import pallas as pl
from jax.experimental.pallas import tpu as pltpu
from jax.sharding import PartitionSpec as P

HEAD = 128
TOKENS = 96
KEYS = 768
neg_big = -1e30


def attention_kernel(heads, blk, order_ref, meta_ref, *refs):
    mine_ref, other_ref, q_ref, do_ref, out_ref, keep_ref, send_ref, kv_ref, kt_s, vt_s, s_s, p_s, dk_s, dv_s = refs
    total = kv_ref.shape[0]
    toks = q_ref.shape[0]
    gt, kc = TOKENS, KEYS
    rows = gt * heads
    sub = gt // blk
    me = meta_ref[0]
    learner = meta_ref[1]
    core = meta_ref[2]
    scale = HEAD ** -0.5
    factor = scale * math.log2(math.e)

    @pl.when(learner == 0)
    def _():
        out_ref[...] = jnp.zeros_like(out_ref)
        keep_ref[...] = jnp.zeros_like(keep_ref)
        send_ref[...] = jnp.zeros_like(send_ref)

    @pl.when(learner == 1)
    def _():
        half = toks
        for r in range(total // half // 2):
            for ref, which in ((mine_ref, core), (other_ref, 1 - core)):
                start = pl.multiple_of((2 * r + which) * half, half)
                kv_ref[pl.ds(start, half), :] = ref[r * half:(r + 1) * half, :]

        for c in range(total // 256):
            part = pl.ds(c * 256, 256)
            kt_s[:, part] = kv_ref[part, :HEAD].T
            vt_s[:, part] = kv_ref[part, HEAD:].T
        dk_s[...] = jnp.zeros_like(dk_s)
        dv_s[...] = jnp.zeros_like(dv_s)

        def stacked(ref, base):
            return jnp.concatenate([ref[pl.ds(base, gt), h * HEAD:(h + 1) * HEAD] for h in range(heads)], axis=0)

        def spread(which, base, value):
            for h in range(heads):
                out_ref[which, pl.ds(base, gt), h * HEAD:(h + 1) * HEAD] = value[h * gt:(h + 1) * gt]

        def group(g, _):
            base = pl.multiple_of(g * gt, gt)
            firsts = [order_ref[me * (toks // blk) + g * sub + s] * blk for s in range(sub)]
            lane = lax.rem(lax.broadcasted_iota(jnp.int32, (1, rows), 1), gt)
            pos = firsts[0] + lane
            for s in range(1, sub):
                pos = jnp.where(lane >= s * blk, firsts[s] + lane - s * blk, pos)
            full = lax.div(firsts[0] + 1, kc)
            last = lax.div(firsts[-1] + blk + kc - 1, kc)
            q = stacked(q_ref, base)
            qt = q.T
            dot_t = stacked(do_ref, base).T

            def scores(masked, c, m):
                part = pl.ds(pl.multiple_of(c * kc, kc), kc)
                s = jnp.dot(kv_ref[part, :HEAD], qt, preferred_element_type=jnp.float32)
                if masked:
                    kpos = c * kc + lax.broadcasted_iota(jnp.int32, (kc, rows), 0)
                    s = jnp.where(kpos <= pos, s, neg_big)
                s_s[part, :] = s
                return jnp.maximum(m, jnp.max(s.reshape(kc // 8, 8, rows), axis=0))

            m = jnp.full((8, rows), neg_big, jnp.float32)
            m = lax.fori_loop(0, full, functools.partial(scores, False), m)
            m = lax.fori_loop(full, last, functools.partial(scores, True), m)
            m = jnp.max(m, axis=0, keepdims=True)

            def weigh(c, carry):
                l, acc = carry
                part = pl.ds(pl.multiple_of(c * kc, kc), kc)
                p = jnp.exp2((s_s[part, :] - m) * factor)
                l = l + jnp.sum(p.reshape(kc // 8, 8, rows), axis=0)
                pb = p.astype(jnp.bfloat16)
                p_s[part, :] = pb
                acc = acc + jnp.dot(vt_s[:, part], pb, preferred_element_type=jnp.float32)
                return l, acc

            l, acc = lax.fori_loop(
                0, last, weigh, (jnp.zeros((8, rows), jnp.float32), jnp.zeros((HEAD, rows), jnp.float32))
            )
            inv = 1.0 / jnp.sum(l, axis=0, keepdims=True)
            ob = (acc * inv).astype(jnp.bfloat16)
            spread(0, base, ob.T)
            dot_f = dot_t.astype(jnp.float32)
            delta = jnp.sum(dot_f * ob.astype(jnp.float32), axis=0, keepdims=True) * inv
            dots = (dot_f * inv).astype(jnp.bfloat16)
            dos = dots.T

            def back(c, acc):
                part = pl.ds(pl.multiple_of(c * kc, kc), kc)
                dp = jnp.dot(kv_ref[part, HEAD:], dots, preferred_element_type=jnp.float32)
                pb = p_s[part, :]
                ds = (pb.astype(jnp.float32) * (dp - delta)).astype(jnp.bfloat16)
                dv_s[part, :] += jnp.dot(pb, dos, preferred_element_type=jnp.float32)
                dk_s[part, :] += jnp.dot(ds, q, preferred_element_type=jnp.float32)
                return acc + jnp.dot(kt_s[:, part], ds, preferred_element_type=jnp.float32)

            acc = lax.fori_loop(0, last, back, jnp.zeros((HEAD, rows), jnp.float32))
            spread(1, base, (acc * scale).astype(jnp.bfloat16).T)
            return 0

        lax.fori_loop(0, toks // gt, group, 0)

        per = toks // blk

        def put(parity, ref, i, _):
            shard = lax.div(i, per) * 2 + parity
            src = pl.ds(pl.multiple_of(order_ref[shard * per + lax.rem(i, per)] * blk, blk), blk)
            dst = pl.ds(pl.multiple_of(i * blk, blk), blk)
            ref[dst, :HEAD] = (dk_s[src, :] * scale).astype(ref.dtype)
            ref[dst, HEAD:] = dv_s[src, :].astype(ref.dtype)
            return 0

        lax.fori_loop(0, total // blk // 2, functools.partial(put, core, keep_ref), 0, unroll=8)
        lax.fori_loop(0, total // blk // 2, functools.partial(put, 1 - core, send_ref), 0, unroll=8)


def attention(order, meta, mine, other, q, do):
    total = mine.shape[0] * 2
    heads = q.shape[1] // HEAD
    rows = TOKENS * heads
    vmem = pl.BlockSpec(memory_space=pltpu.VMEM)
    smem = pl.BlockSpec(memory_space=pltpu.SMEM)
    return pl.pallas_call(
        functools.partial(attention_kernel, heads, total // order.shape[0]),
        out_shape=(
            jax.ShapeDtypeStruct((2,) + q.shape, jnp.bfloat16),
            jax.ShapeDtypeStruct((total // 2, 2 * HEAD), jnp.float32),
            jax.ShapeDtypeStruct((total // 2, 2 * HEAD), jnp.bfloat16),
        ),
        in_specs=[smem, smem] + [vmem] * 4,
        out_specs=(vmem, vmem, vmem),
        scratch_shapes=[
            pltpu.VMEM((total, 2 * HEAD), jnp.bfloat16),
            pltpu.VMEM((HEAD, total), jnp.bfloat16),
            pltpu.VMEM((HEAD, total), jnp.bfloat16),
            pltpu.VMEM((total, rows), jnp.float32),
            pltpu.VMEM((total, rows), jnp.bfloat16),
            pltpu.VMEM((total, HEAD), jnp.float32),
            pltpu.VMEM((total, HEAD), jnp.float32),
        ],
        compiler_params=pltpu.CompilerParams(vmem_limit_bytes=48 * 2**20),
    )(order, meta, mine, other, q, do)


def runs_kernel(lengths_ref, z_ref, cached_ref, new_ref, owner_ref, *refs):
    run_refs, sems = refs[:-1], refs[-1]
    ring = len(run_refs)
    run = run_refs[0].shape[0]
    row_count, total, _ = cached_ref.shape
    finished = jnp.int32(0)
    for r in range(lengths_ref.shape[0]):
        finished = jnp.where(lengths_ref[r] == total, r, finished)
    picked = lax.rem(finished, row_count)
    owner_ref[0] = lax.div(finished, row_count)
    copies = []
    for step, ref in enumerate(run_refs):
        start = pl.multiple_of(lax.rem(z_ref[0] + step, ring) * run, run)
        copies.append(pltpu.make_async_copy(cached_ref.at[picked, pl.ds(start, run)], ref, sems.at[step]))
    for copy in copies:
        copy.start()
    new_row = new_ref[0:1, :]
    for r in range(1, row_count):
        new_row = jnp.where(picked == r, new_ref[r:r + 1, :], new_row)
    for copy in copies:
        copy.wait()
    for step, ref in enumerate(run_refs):
        @pl.when(lax.rem(z_ref[0] + step, ring) == ring - 1)
        def _(ref=ref):
            at = lax.broadcasted_iota(jnp.int32, (16, ref.shape[1]), 0)
            tail = pl.ds(run - 16, 16)
            ref[tail, :] = jnp.where(at == 15, new_row, ref[tail, :])


def finished_runs(lengths, z_index, cached, new_pairs, ring):
    total, width = cached.shape[1:]
    vmem = pl.BlockSpec(memory_space=pltpu.VMEM)
    smem = pl.BlockSpec(memory_space=pltpu.SMEM)
    return pl.pallas_call(
        runs_kernel,
        out_shape=[jax.ShapeDtypeStruct((1,), jnp.int32)]
        + [jax.ShapeDtypeStruct((total // ring, width), cached.dtype)] * ring,
        in_specs=[smem, smem, pl.BlockSpec(memory_space=pl.ANY), vmem],
        out_specs=[smem] + [vmem] * ring,
        scratch_shapes=[pltpu.SemaphoreType.DMA((ring,))],
        compiler_params=pltpu.CompilerParams(vmem_limit_bytes=16 * 2**20),
    )(lengths, z_index.reshape(1), cached, new_pairs)


def decode_rows(operands):
    cached, new_pair, final_query, row_lengths, weight_rows = operands
    row_count, total, _ = cached.shape
    heads = final_query.shape[1] // HEAD
    positions = jnp.arange(total, dtype=jnp.int32)
    is_last = (positions[None, :] == (row_lengths - 1)[:, None])[:, None, :]
    query = final_query.reshape(row_count, heads, HEAD)
    scores = jnp.einsum("rgd,rld->rgl", query, cached[:, :, :HEAD], preferred_element_type=jnp.float32)
    new_score = jnp.einsum("rgd,rd->rg", query, new_pair[:, :HEAD], preferred_element_type=jnp.float32)
    scores = jnp.where(is_last, new_score[:, :, None], scores) * HEAD ** -0.5
    valid = (positions[None, :] < row_lengths[:, None])[:, None, :]
    scores = jnp.where(valid, scores, neg_big)
    weights = jnp.where(valid, jnp.exp(scores - jnp.max(scores, axis=-1, keepdims=True)), 0.0)
    rounded = weights.astype(jnp.bfloat16)
    old = jnp.where(is_last, jnp.zeros_like(rounded), rounded)
    new = jnp.sum(jnp.where(is_last, rounded.astype(jnp.float32), 0.0), axis=-1)
    mixed = jnp.einsum("rgl,rld->rgd", old, cached[:, :, HEAD:], preferred_element_type=jnp.float32)
    mixed = mixed + new[:, :, None] * new_pair[:, None, HEAD:].astype(jnp.float32)
    attended = (mixed / jnp.sum(weights, axis=-1)[..., None]).astype(jnp.bfloat16)
    return jnp.dot(attended.reshape(row_count, heads * HEAD), weight_rows, preferred_element_type=jnp.float32)


def shards(
    key_value_cache, new_kv, final_query, out_weight, lengths, block_plan, queries, output_gradient
):
    grp_index = lax.axis_index("grp")
    ctx_index = lax.axis_index("ctx")
    ctx_size = lax.axis_size("ctx")
    tp_size = lax.axis_size("tp")
    ring = ctx_size // 2
    z_index, column = ctx_index >> 1, ctx_index & 1
    core = lax.axis_index("tp") & 1

    def route(groups, move, stay=False):
        pairs = []
        for at in itertools.product(groups, range(ring), range(2), range(tp_size // 2), range(2)):
            to = move(*at)
            if stay or to != at:
                pairs.append(tuple((((g * ring + z) * 2 + h) * tp_size) + y * 2 + c for g, z, h, y, c in (at, to)))
        return pairs

    def sent(x, pairs):
        return lax.ppermute(x, ("grp", "ctx", "tp"), pairs)

    swap = route((1,), lambda g, z, h, y, c: (g, z, c, y, h))
    swap_all = route((1,), lambda g, z, h, y, c: (g, z, c, y, h), True)
    cores = route((0, 1), lambda g, z, h, y, c: (g, z, h, y, 1 - c))
    across = route((0,), lambda g, z, h, y, c: (1, z, c, y, h))

    cached = key_value_cache[0]
    row_count, total, width = cached.shape
    run = total // ring
    half = run // 2
    owner, *runs = finished_runs(lengths, z_index, cached, new_kv[0], ring)
    owner = owner[0]
    owner_z = owner >> 1
    distance = lax.rem(z_index + ring - owner_z, ring)

    def scatter_from(first):
        def scatter(parts):
            got = parts[0]
            for step in range(1, ring):
                pairs = [
                    (z * 2 + h, (z + step) % ring * 2 + h) for z in range(first, ring, classes) for h in range(2)
                ]
                arrived = lax.ppermute(parts[step], ("grp", "ctx"), pairs)
                got = jnp.where(distance == step, arrived, got)
            return got

        return scatter

    classes = ring // 2
    held = lax.switch(lax.rem(owner_z, classes), [scatter_from(first) for first in range(classes)], runs)

    stays = column == core
    query_rows = sent(queries[0], swap_all)
    gradient_rows = sent(output_gradient[0], swap)
    gradient_rows = jnp.where(stays, output_gradient[0], gradient_rows)
    landed = sent(held, across)
    landed, query_rows, gradient_rows, order = lax.optimization_barrier(
        (landed, query_rows, gradient_rows, jnp.argsort(block_plan, stable=True).astype(jnp.int32))
    )
    low, high = landed[:half], landed[half:]
    handed = sent(jnp.where(core == 0, high, low), cores)
    own = jnp.where(core == (owner & 1), jnp.where(core == 0, low, high), handed)
    columns = [list(range(h, ctx_size, 2)) for h in range(2)]
    mine = lax.all_gather(own, "ctx", axis=0, tiled=True, axis_index_groups=columns)
    other = sent(mine, cores)

    meta = jnp.stack([z_index * 2 + core, grp_index, core]).astype(jnp.int32)
    result_rows, kept, passed = attention(order, meta, mine, other, query_rows, gradient_rows)
    summed = (kept + sent(passed, cores).astype(jnp.float32)).astype(jnp.bfloat16)
    spread = lax.all_to_all(
        summed.reshape(ring, total // ctx_size, width), "ctx", 0, 0, axis_index_groups=columns
    )
    returned = sent(result_rows, swap)
    attn_out = jnp.where(stays, result_rows[0], returned[0])
    grad_query = jnp.where(stays, result_rows[1], returned[1])
    spread, attn_out, grad_query = lax.optimization_barrier((spread, attn_out, grad_query))
    grads = jnp.sum(spread.astype(jnp.float32), axis=0).astype(jnp.bfloat16)
    grad_pairs = sent(grads, swap_all)

    row_lengths = lax.dynamic_slice_in_dim(lengths, ctx_index * row_count, row_count)
    held_query, _ = lax.optimization_barrier((final_query[0], held))
    partial_out = lax.cond(
        grp_index == 0,
        decode_rows,
        lambda operands: jnp.zeros((row_count, out_weight.shape[2]), jnp.float32),
        (cached, new_kv[0], held_query, row_lengths, out_weight[0]),
    )
    partial_out = partial_out + sent(partial_out, cores)
    count = tp_size // 2
    onward = route((0,), lambda g, z, h, y, c: (g, z, h, (y + 1) % count, c))
    terms = [partial_out]
    for _ in range(count - 1):
        terms.append(sent(terms[-1], onward))
    y_index = lax.axis_index("tp") >> 1
    partial_out = jnp.zeros_like(partial_out)
    for y in range(count):
        back = (y_index - y) & (count - 1)
        partial_out = partial_out + sum(jnp.where(back == step, terms[step], 0.0) for step in range(count))
    decoded = partial_out.astype(jnp.bfloat16)
    return (decoded[None], attn_out[None], grad_query[None], grad_pairs[None])


def solution(mesh):
    return jax.shard_map(
        shards,
        mesh=mesh,
        in_specs=(
            P("grp", "ctx", None, "tp"),
            P("grp", "ctx", "tp"),
            P("grp", "ctx", "tp"),
            P("grp", "tp", None),
            P(),
            P(),
            P("grp", "ctx", "tp"),
            P("grp", "ctx", "tp"),
        ),
        out_specs=(
            P("grp", "ctx", None),
            P("grp", "ctx", "tp"),
            P("grp", "ctx", "tp"),
            P("grp", "ctx", "tp"),
        ),
        check_vma=False,
    )
```

```python
import functools
import itertools
import math

import jax
import jax.numpy as jnp
from jax import lax
from jax.experimental import pallas as pl
from jax.experimental.pallas import tpu as pltpu
from jax.sharding import PartitionSpec as P

HEAD = 128
TOKENS = 96
KEYS = 768
neg_big = -1e30


def attention_kernel(heads, blk, order_ref, meta_ref, *refs):
    mine_ref, other_ref, q_ref, do_ref, out_ref, keep_ref, send_ref, kv_ref, kt_s, vt_s, s_s, p_s, dk_s, dv_s, dq_s, o_s = refs
    total = kv_ref.shape[0]
    toks = q_ref.shape[0]
    gt, kc = TOKENS, KEYS
    rows = gt * heads
    sub = gt // blk
    me = meta_ref[0]
    learner = meta_ref[1]
    core = meta_ref[2]
    scale = HEAD ** -0.5
    factor = scale * math.log2(math.e)

    @pl.when(learner == 0)
    def _():
        out_ref[...] = jnp.zeros_like(out_ref)
        keep_ref[...] = jnp.zeros_like(keep_ref)
        send_ref[...] = jnp.zeros_like(send_ref)

    @pl.when(learner == 1)
    def _():
        half = toks
        for r in range(total // half // 2):
            for ref, which in ((mine_ref, core), (other_ref, 1 - core)):
                start = pl.multiple_of((2 * r + which) * half, half)
                kv_ref[pl.ds(start, half), :] = ref[r * half:(r + 1) * half, :]

        for c in range(total // 256):
            part = pl.ds(c * 256, 256)
            kt_s[:, part] = kv_ref[part, :HEAD].T
            vt_s[:, part] = kv_ref[part, HEAD:].T
        dk_s[...] = jnp.zeros_like(dk_s)
        dv_s[...] = jnp.zeros_like(dv_s)

        def stacked(ref, base):
            return jnp.concatenate([ref[pl.ds(base, gt), h * HEAD:(h + 1) * HEAD] for h in range(heads)], axis=0)

        def spread(which, base, value):
            for h in range(heads):
                out_ref[which, pl.ds(base, gt), h * HEAD:(h + 1) * HEAD] = value[h * gt:(h + 1) * gt]

        def group(g, _):
            base = pl.multiple_of(g * gt, gt)
            firsts = [order_ref[me * (toks // blk) + g * sub + s] * blk for s in range(sub)]
            lane = lax.rem(lax.broadcasted_iota(jnp.int32, (1, rows), 1), gt)
            pos = firsts[0] + lane
            for s in range(1, sub):
                pos = jnp.where(lane >= s * blk, firsts[s] + lane - s * blk, pos)
            full = lax.div(firsts[0] + 1, kc)
            last = lax.div(firsts[-1] + blk + kc - 1, kc)
            q = stacked(q_ref, base)
            qt = q.T
            dot_t = stacked(do_ref, base).T

            def scores(masked, c, m):
                part = pl.ds(pl.multiple_of(c * kc, kc), kc)
                s = jnp.dot(kv_ref[part, :HEAD], qt, preferred_element_type=jnp.float32)
                if masked:
                    kpos = c * kc + lax.broadcasted_iota(jnp.int32, (kc, rows), 0)
                    s = jnp.where(kpos <= pos, s, neg_big)
                s_s[part, :] = s
                return jnp.maximum(m, jnp.max(s.reshape(kc // 8, 8, rows), axis=0))

            m = jnp.full((8, rows), neg_big, jnp.float32)
            m = lax.fori_loop(0, full, functools.partial(scores, False), m)
            m = lax.fori_loop(full, last, functools.partial(scores, True), m)
            m = jnp.max(m, axis=0, keepdims=True)

            def weigh(c, carry):
                l = carry
                part = pl.ds(pl.multiple_of(c * kc, kc), kc)
                p = jnp.exp2((s_s[part, :] - m) * factor)
                l = l + jnp.sum(p.reshape(kc // 8, 8, rows), axis=0)
                pb = p.astype(jnp.bfloat16)
                p_s[part, :] = pb
                o_s[...] += jnp.dot(vt_s[:, part], pb, preferred_element_type=jnp.float32)
                return l

            o_s[...] = jnp.zeros_like(o_s)
            l = lax.fori_loop(0, last, weigh, jnp.zeros((8, rows), jnp.float32))
            acc = o_s[...]
            inv = 1.0 / jnp.sum(l, axis=0, keepdims=True)
            ob = (acc * inv).astype(jnp.bfloat16)
            spread(0, base, ob.T)
            dot_f = dot_t.astype(jnp.float32)
            delta = jnp.sum(dot_f * ob.astype(jnp.float32), axis=0, keepdims=True) * inv
            dots = (dot_f * inv).astype(jnp.bfloat16)
            dos = dots.T

            def back(c, acc):
                part = pl.ds(pl.multiple_of(c * kc, kc), kc)
                dp = jnp.dot(kv_ref[part, HEAD:], dots, preferred_element_type=jnp.float32)
                pb = p_s[part, :]
                ds = (pb.astype(jnp.float32) * (dp - delta)).astype(jnp.bfloat16)
                dv_s[part, :] += jnp.dot(pb, dos, preferred_element_type=jnp.float32)
                dk_s[part, :] += jnp.dot(ds, q, preferred_element_type=jnp.float32)
                dq_s[...] += jnp.dot(kt_s[:, part], ds, preferred_element_type=jnp.float32)
                return acc

            dq_s[...] = jnp.zeros_like(dq_s)
            lax.fori_loop(0, last, back, 0)
            acc = dq_s[...]
            spread(1, base, (acc * scale).astype(jnp.bfloat16).T)
            return 0

        lax.fori_loop(0, toks // gt, group, 0)

        per = toks // blk

        def put(parity, ref, i, _):
            shard = lax.div(i, per) * 2 + parity
            src = pl.ds(pl.multiple_of(order_ref[shard * per + lax.rem(i, per)] * blk, blk), blk)
            dst = pl.ds(pl.multiple_of(i * blk, blk), blk)
            ref[dst, :HEAD] = (dk_s[src, :] * scale).astype(ref.dtype)
            ref[dst, HEAD:] = dv_s[src, :].astype(ref.dtype)
            return 0

        lax.fori_loop(0, total // blk // 2, functools.partial(put, core, keep_ref), 0, unroll=8)
        lax.fori_loop(0, total // blk // 2, functools.partial(put, 1 - core, send_ref), 0, unroll=8)


def attention(order, meta, mine, other, q, do):
    total = mine.shape[0] * 2
    heads = q.shape[1] // HEAD
    rows = TOKENS * heads
    vmem = pl.BlockSpec(memory_space=pltpu.VMEM)
    smem = pl.BlockSpec(memory_space=pltpu.SMEM)
    return pl.pallas_call(
        functools.partial(attention_kernel, heads, total // order.shape[0]),
        out_shape=(
            jax.ShapeDtypeStruct((2,) + q.shape, jnp.bfloat16),
            jax.ShapeDtypeStruct((total // 2, 2 * HEAD), jnp.float32),
            jax.ShapeDtypeStruct((total // 2, 2 * HEAD), jnp.bfloat16),
        ),
        in_specs=[smem, smem] + [vmem] * 4,
        out_specs=(vmem, vmem, vmem),
        scratch_shapes=[
            pltpu.VMEM((total, 2 * HEAD), jnp.bfloat16),
            pltpu.VMEM((HEAD, total), jnp.bfloat16),
            pltpu.VMEM((HEAD, total), jnp.bfloat16),
            pltpu.VMEM((total, rows), jnp.float32),
            pltpu.VMEM((total, rows), jnp.bfloat16),
            pltpu.VMEM((total, HEAD), jnp.float32),
            pltpu.VMEM((total, HEAD), jnp.float32),
            pltpu.VMEM((HEAD, rows), jnp.float32),
            pltpu.VMEM((HEAD, rows), jnp.float32),
        ],
        compiler_params=pltpu.CompilerParams(vmem_limit_bytes=48 * 2**20),
    )(order, meta, mine, other, q, do)


def runs_kernel(lengths_ref, z_ref, cached_ref, new_ref, owner_ref, *refs):
    run_refs, sems = refs[:-1], refs[-1]
    ring = len(run_refs)
    run = run_refs[0].shape[0]
    row_count, total, _ = cached_ref.shape
    finished = jnp.int32(0)
    for r in range(lengths_ref.shape[0]):
        finished = jnp.where(lengths_ref[r] == total, r, finished)
    picked = lax.rem(finished, row_count)
    owner_ref[0] = lax.div(finished, row_count)
    copies = []
    for step, ref in enumerate(run_refs):
        start = pl.multiple_of(lax.rem(z_ref[0] + step, ring) * run, run)
        copies.append(pltpu.make_async_copy(cached_ref.at[picked, pl.ds(start, run)], ref, sems.at[step]))
    for copy in copies:
        copy.start()
    new_row = new_ref[0:1, :]
    for r in range(1, row_count):
        new_row = jnp.where(picked == r, new_ref[r:r + 1, :], new_row)
    for copy in copies:
        copy.wait()
    for step, ref in enumerate(run_refs):
        @pl.when(lax.rem(z_ref[0] + step, ring) == ring - 1)
        def _(ref=ref):
            at = lax.broadcasted_iota(jnp.int32, (16, ref.shape[1]), 0)
            tail = pl.ds(run - 16, 16)
            ref[tail, :] = jnp.where(at == 15, new_row, ref[tail, :])


def finished_runs(lengths, z_index, cached, new_pairs, ring):
    total, width = cached.shape[1:]
    vmem = pl.BlockSpec(memory_space=pltpu.VMEM)
    smem = pl.BlockSpec(memory_space=pltpu.SMEM)
    return pl.pallas_call(
        runs_kernel,
        out_shape=[jax.ShapeDtypeStruct((1,), jnp.int32)]
        + [jax.ShapeDtypeStruct((total // ring, width), cached.dtype)] * ring,
        in_specs=[smem, smem, pl.BlockSpec(memory_space=pl.ANY), vmem],
        out_specs=[smem] + [vmem] * ring,
        scratch_shapes=[pltpu.SemaphoreType.DMA((ring,))],
        compiler_params=pltpu.CompilerParams(vmem_limit_bytes=16 * 2**20),
    )(lengths, z_index.reshape(1), cached, new_pairs)


def decode_rows(operands):
    cached, new_pair, final_query, row_lengths, weight_rows = operands
    row_count, total, _ = cached.shape
    heads = final_query.shape[1] // HEAD
    positions = jnp.arange(total, dtype=jnp.int32)
    is_last = (positions[None, :] == (row_lengths - 1)[:, None])[:, None, :]
    query = final_query.reshape(row_count, heads, HEAD)
    scores = jnp.einsum("rgd,rld->rgl", query, cached[:, :, :HEAD], preferred_element_type=jnp.float32)
    new_score = jnp.einsum("rgd,rd->rg", query, new_pair[:, :HEAD], preferred_element_type=jnp.float32)
    scores = jnp.where(is_last, new_score[:, :, None], scores) * HEAD ** -0.5
    valid = (positions[None, :] < row_lengths[:, None])[:, None, :]
    scores = jnp.where(valid, scores, neg_big)
    weights = jnp.where(valid, jnp.exp(scores - jnp.max(scores, axis=-1, keepdims=True)), 0.0)
    rounded = weights.astype(jnp.bfloat16)
    old = jnp.where(is_last, jnp.zeros_like(rounded), rounded)
    new = jnp.sum(jnp.where(is_last, rounded.astype(jnp.float32), 0.0), axis=-1)
    mixed = jnp.einsum("rgl,rld->rgd", old, cached[:, :, HEAD:], preferred_element_type=jnp.float32)
    mixed = mixed + new[:, :, None] * new_pair[:, None, HEAD:].astype(jnp.float32)
    attended = (mixed / jnp.sum(weights, axis=-1)[..., None]).astype(jnp.bfloat16)
    return jnp.dot(attended.reshape(row_count, heads * HEAD), weight_rows, preferred_element_type=jnp.float32)


def shards(
    key_value_cache, new_kv, final_query, out_weight, lengths, block_plan, queries, output_gradient
):
    grp_index = lax.axis_index("grp")
    ctx_index = lax.axis_index("ctx")
    ctx_size = lax.axis_size("ctx")
    tp_size = lax.axis_size("tp")
    ring = ctx_size // 2
    z_index, column = ctx_index >> 1, ctx_index & 1
    core = lax.axis_index("tp") & 1

    def route(groups, move, stay=False):
        pairs = []
        for at in itertools.product(groups, range(ring), range(2), range(tp_size // 2), range(2)):
            to = move(*at)
            if stay or to != at:
                pairs.append(tuple((((g * ring + z) * 2 + h) * tp_size) + y * 2 + c for g, z, h, y, c in (at, to)))
        return pairs

    def sent(x, pairs):
        return lax.ppermute(x, ("grp", "ctx", "tp"), pairs)

    swap = route((1,), lambda g, z, h, y, c: (g, z, c, y, h))
    swap_all = route((1,), lambda g, z, h, y, c: (g, z, c, y, h), True)
    cores = route((0, 1), lambda g, z, h, y, c: (g, z, h, y, 1 - c))
    across = route((0,), lambda g, z, h, y, c: (1, z, c, y, h))

    cached = key_value_cache[0]
    row_count, total, width = cached.shape
    run = total // ring
    half = run // 2
    owner, *runs = finished_runs(lengths, z_index, cached, new_kv[0], ring)
    owner = owner[0]
    owner_z = owner >> 1
    distance = lax.rem(z_index + ring - owner_z, ring)

    def scatter_from(first):
        def scatter(parts):
            got = parts[0]
            for step in sorted(range(1, ring), key=lambda step: (-abs(step - ring // 2), -step)):
                pairs = [
                    (z * 2 + h, (z + step) % ring * 2 + h) for z in range(first, ring, classes) for h in range(2)
                ]
                arrived = lax.ppermute(parts[step], ("grp", "ctx"), pairs)
                got = jnp.where(distance == step, arrived, got)
            return got

        return scatter

    classes = ring // 2
    held = lax.switch(lax.rem(owner_z, classes), [scatter_from(first) for first in range(classes)], runs)

    stays = column == core
    query_rows = sent(queries[0], swap_all)
    gradient_rows = sent(output_gradient[0], swap)
    gradient_rows = jnp.where(stays, output_gradient[0], gradient_rows)
    landed = sent(held, across)
    landed, query_rows, gradient_rows, order = lax.optimization_barrier(
        (landed, query_rows, gradient_rows, jnp.argsort(block_plan, stable=True).astype(jnp.int32))
    )
    low, high = landed[:half], landed[half:]
    handed = sent(jnp.where(core == 0, high, low), cores)
    own = jnp.where(core == (owner & 1), jnp.where(core == 0, low, high), handed)
    columns = [list(range(h, ctx_size, 2)) for h in range(2)]
    mine = lax.all_gather(own, "ctx", axis=0, tiled=True, axis_index_groups=columns)
    other = sent(mine, cores)

    meta = jnp.stack([z_index * 2 + core, grp_index, core]).astype(jnp.int32)
    result_rows, kept, passed = attention(order, meta, mine, other, query_rows, gradient_rows)
    summed = (kept + sent(passed, cores).astype(jnp.float32)).astype(jnp.bfloat16)
    spread = lax.all_to_all(
        summed.reshape(ring, total // ctx_size, width), "ctx", 0, 0, axis_index_groups=columns
    )
    returned = sent(result_rows, swap)
    attn_out = jnp.where(stays, result_rows[0], returned[0])
    grad_query = jnp.where(stays, result_rows[1], returned[1])
    spread, attn_out, grad_query = lax.optimization_barrier((spread, attn_out, grad_query))
    grads = jnp.sum(spread.astype(jnp.float32), axis=0).astype(jnp.bfloat16)
    grad_pairs = sent(grads, swap_all)

    row_lengths = lax.dynamic_slice_in_dim(lengths, ctx_index * row_count, row_count)
    held_query, _ = lax.optimization_barrier((final_query[0], held))
    partial_out = lax.cond(
        grp_index == 0,
        decode_rows,
        lambda operands: jnp.zeros((row_count, out_weight.shape[2]), jnp.float32),
        (cached, new_kv[0], held_query, row_lengths, out_weight[0]),
    )
    partial_out = partial_out + sent(partial_out, cores)
    count = tp_size // 2
    onward = route((0,), lambda g, z, h, y, c: (g, z, h, (y + 1) % count, c))
    terms = [partial_out]
    for _ in range(count - 1):
        terms.append(sent(terms[-1], onward))
    y_index = lax.axis_index("tp") >> 1
    partial_out = jnp.zeros_like(partial_out)
    for y in range(count):
        back = (y_index - y) & (count - 1)
        partial_out = partial_out + sum(jnp.where(back == step, terms[step], 0.0) for step in range(count))
    decoded = partial_out.astype(jnp.bfloat16)
    return (decoded[None], attn_out[None], grad_query[None], grad_pairs[None])


def solution(mesh):
    return jax.shard_map(
        shards,
        mesh=mesh,
        in_specs=(
            P("grp", "ctx", None, "tp"),
            P("grp", "ctx", "tp"),
            P("grp", "ctx", "tp"),
            P("grp", "tp", None),
            P(),
            P(),
            P("grp", "ctx", "tp"),
            P("grp", "ctx", "tp"),
        ),
        out_specs=(
            P("grp", "ctx", None),
            P("grp", "ctx", "tp"),
            P("grp", "ctx", "tp"),
            P("grp", "ctx", "tp"),
        ),
        check_vma=False,
    )
```

```python
import functools
import itertools
import math

import jax
import jax.numpy as jnp
from jax import lax
from jax.experimental import pallas as pl
from jax.experimental.pallas import tpu as pltpu
from jax.sharding import PartitionSpec as P

HEAD = 128
TOKENS = 96
KEYS = 768
neg_big = -1e30


def attention_kernel(heads, blk, order_ref, meta_ref, *refs):
    mine_ref, other_ref, q_ref, do_ref, out_ref, keep_ref, send_ref, kv_ref, kt_s, vt_s, s_s, p_s, dk_s, dv_s, dq_s, o_s = refs
    total = kv_ref.shape[0]
    toks = q_ref.shape[0]
    gt, kc = TOKENS, KEYS
    rows = gt * heads
    sub = gt // blk
    me = meta_ref[0]
    learner = meta_ref[1]
    core = meta_ref[2]
    scale = HEAD ** -0.5
    factor = scale * math.log2(math.e)

    @pl.when(learner == 0)
    def _():
        out_ref[...] = jnp.zeros_like(out_ref)
        keep_ref[...] = jnp.zeros_like(keep_ref)
        send_ref[...] = jnp.zeros_like(send_ref)

    @pl.when(learner == 1)
    def _():
        half = toks
        ring = total // half // 2
        z = lax.div(me, 2)
        for r in range(ring):
            run = lax.rem(z + ring + (r // 2 if r % 2 == 0 else -(r + 1) // 2), ring)
            if r == ring - 1:
                run = lax.rem(z + ring // 2, ring)
            for ref, which in ((mine_ref, core), (other_ref, 1 - core)):
                start = pl.multiple_of((2 * run + which) * half, half)
                kv_ref[pl.ds(start, half), :] = ref[r * half:(r + 1) * half, :]

        for c in range(total // 256):
            part = pl.ds(c * 256, 256)
            kt_s[:, part] = kv_ref[part, :HEAD].T
            vt_s[:, part] = kv_ref[part, HEAD:].T
        dk_s[...] = jnp.zeros_like(dk_s)
        dv_s[...] = jnp.zeros_like(dv_s)

        def stacked(ref, base):
            return jnp.concatenate([ref[pl.ds(base, gt), h * HEAD:(h + 1) * HEAD] for h in range(heads)], axis=0)

        def spread(which, base, value):
            for h in range(heads):
                out_ref[which, pl.ds(base, gt), h * HEAD:(h + 1) * HEAD] = value[h * gt:(h + 1) * gt]

        def group(g, _):
            base = pl.multiple_of(g * gt, gt)
            firsts = [order_ref[me * (toks // blk) + g * sub + s] * blk for s in range(sub)]
            lane = lax.rem(lax.broadcasted_iota(jnp.int32, (1, rows), 1), gt)
            pos = firsts[0] + lane
            for s in range(1, sub):
                pos = jnp.where(lane >= s * blk, firsts[s] + lane - s * blk, pos)
            full = lax.div(firsts[0] + 1, kc)
            last = lax.div(firsts[-1] + blk + kc - 1, kc)
            q = stacked(q_ref, base)
            qt = q.T
            dot_t = stacked(do_ref, base).T

            def scores(masked, c, m):
                part = pl.ds(pl.multiple_of(c * kc, kc), kc)
                s = jnp.dot(kv_ref[part, :HEAD], qt, preferred_element_type=jnp.float32)
                if masked:
                    kpos = c * kc + lax.broadcasted_iota(jnp.int32, (kc, rows), 0)
                    s = jnp.where(kpos <= pos, s, neg_big)
                s_s[part, :] = s
                return jnp.maximum(m, jnp.max(s.reshape(kc // 8, 8, rows), axis=0))

            m = jnp.full((8, rows), neg_big, jnp.float32)
            m = lax.fori_loop(0, full, functools.partial(scores, False), m)
            m = lax.fori_loop(full, last, functools.partial(scores, True), m)
            m = jnp.max(m, axis=0, keepdims=True)

            def weigh(c, carry):
                l = carry
                part = pl.ds(pl.multiple_of(c * kc, kc), kc)
                p = jnp.exp2((s_s[part, :] - m) * factor)
                l = l + jnp.sum(p.reshape(kc // 8, 8, rows), axis=0)
                pb = p.astype(jnp.bfloat16)
                p_s[part, :] = pb
                o_s[...] += jnp.dot(vt_s[:, part], pb, preferred_element_type=jnp.float32)
                return l

            o_s[...] = jnp.zeros_like(o_s)
            l = lax.fori_loop(0, last, weigh, jnp.zeros((8, rows), jnp.float32))
            acc = o_s[...]
            inv = 1.0 / jnp.sum(l, axis=0, keepdims=True)
            ob = (acc * inv).astype(jnp.bfloat16)
            spread(0, base, ob.T)
            dot_f = dot_t.astype(jnp.float32)
            delta = jnp.sum(dot_f * ob.astype(jnp.float32), axis=0, keepdims=True) * inv
            dots = (dot_f * inv).astype(jnp.bfloat16)
            dos = dots.T

            def back(c, acc):
                part = pl.ds(pl.multiple_of(c * kc, kc), kc)
                dp = jnp.dot(kv_ref[part, HEAD:], dots, preferred_element_type=jnp.float32)
                pb = p_s[part, :]
                ds = (pb.astype(jnp.float32) * (dp - delta)).astype(jnp.bfloat16)
                dv_s[part, :] += jnp.dot(pb, dos, preferred_element_type=jnp.float32)
                dk_s[part, :] += jnp.dot(ds, q, preferred_element_type=jnp.float32)
                dq_s[...] += jnp.dot(kt_s[:, part], ds, preferred_element_type=jnp.float32)
                return acc

            dq_s[...] = jnp.zeros_like(dq_s)
            lax.fori_loop(0, last, back, 0)
            acc = dq_s[...]
            spread(1, base, (acc * scale).astype(jnp.bfloat16).T)
            return 0

        lax.fori_loop(0, toks // gt, group, 0)

        per = toks // blk

        def put(parity, ref, i, _):
            shard = lax.div(i, per) * 2 + parity
            src = pl.ds(pl.multiple_of(order_ref[shard * per + lax.rem(i, per)] * blk, blk), blk)
            dst = pl.ds(pl.multiple_of(i * blk, blk), blk)
            ref[dst, :HEAD] = (dk_s[src, :] * scale).astype(ref.dtype)
            ref[dst, HEAD:] = dv_s[src, :].astype(ref.dtype)
            return 0

        lax.fori_loop(0, total // blk // 2, functools.partial(put, core, keep_ref), 0, unroll=8)
        lax.fori_loop(0, total // blk // 2, functools.partial(put, 1 - core, send_ref), 0, unroll=8)


def attention(order, meta, mine, other, q, do):
    total = mine.shape[0] * 2
    heads = q.shape[1] // HEAD
    rows = TOKENS * heads
    vmem = pl.BlockSpec(memory_space=pltpu.VMEM)
    smem = pl.BlockSpec(memory_space=pltpu.SMEM)
    return pl.pallas_call(
        functools.partial(attention_kernel, heads, total // order.shape[0]),
        out_shape=(
            jax.ShapeDtypeStruct((2,) + q.shape, jnp.bfloat16),
            jax.ShapeDtypeStruct((total // 2, 2 * HEAD), jnp.float32),
            jax.ShapeDtypeStruct((total // 2, 2 * HEAD), jnp.bfloat16),
        ),
        in_specs=[smem, smem] + [vmem] * 4,
        out_specs=(vmem, vmem, vmem),
        scratch_shapes=[
            pltpu.VMEM((total, 2 * HEAD), jnp.bfloat16),
            pltpu.VMEM((HEAD, total), jnp.bfloat16),
            pltpu.VMEM((HEAD, total), jnp.bfloat16),
            pltpu.VMEM((total, rows), jnp.float32),
            pltpu.VMEM((total, rows), jnp.bfloat16),
            pltpu.VMEM((total, HEAD), jnp.float32),
            pltpu.VMEM((total, HEAD), jnp.float32),
            pltpu.VMEM((HEAD, rows), jnp.float32),
            pltpu.VMEM((HEAD, rows), jnp.float32),
        ],
        compiler_params=pltpu.CompilerParams(vmem_limit_bytes=48 * 2**20),
    )(order, meta, mine, other, q, do)


def runs_kernel(lengths_ref, z_ref, cached_ref, new_ref, owner_ref, *refs):
    run_refs, sems = refs[:-1], refs[-1]
    ring = len(run_refs)
    run = run_refs[0].shape[0]
    row_count, total, _ = cached_ref.shape
    finished = jnp.int32(0)
    for r in range(lengths_ref.shape[0]):
        finished = jnp.where(lengths_ref[r] == total, r, finished)
    picked = lax.rem(finished, row_count)
    owner_ref[0] = lax.div(finished, row_count)
    copies = []
    for step, ref in enumerate(run_refs):
        start = pl.multiple_of(lax.rem(z_ref[0] + step, ring) * run, run)
        copies.append(pltpu.make_async_copy(cached_ref.at[picked, pl.ds(start, run)], ref, sems.at[step]))
    for copy in copies:
        copy.start()
    new_row = new_ref[0:1, :]
    for r in range(1, row_count):
        new_row = jnp.where(picked == r, new_ref[r:r + 1, :], new_row)
    for copy in copies:
        copy.wait()
    for step, ref in enumerate(run_refs):
        @pl.when(lax.rem(z_ref[0] + step, ring) == ring - 1)
        def _(ref=ref):
            at = lax.broadcasted_iota(jnp.int32, (16, ref.shape[1]), 0)
            tail = pl.ds(run - 16, 16)
            ref[tail, :] = jnp.where(at == 15, new_row, ref[tail, :])


def finished_runs(lengths, z_index, cached, new_pairs, ring):
    total, width = cached.shape[1:]
    vmem = pl.BlockSpec(memory_space=pltpu.VMEM)
    smem = pl.BlockSpec(memory_space=pltpu.SMEM)
    return pl.pallas_call(
        runs_kernel,
        out_shape=[jax.ShapeDtypeStruct((1,), jnp.int32)]
        + [jax.ShapeDtypeStruct((total // ring, width), cached.dtype)] * ring,
        in_specs=[smem, smem, pl.BlockSpec(memory_space=pl.ANY), vmem],
        out_specs=[smem] + [vmem] * ring,
        scratch_shapes=[pltpu.SemaphoreType.DMA((ring,))],
        compiler_params=pltpu.CompilerParams(vmem_limit_bytes=16 * 2**20),
    )(lengths, z_index.reshape(1), cached, new_pairs)


def decode_rows(operands):
    cached, new_pair, final_query, row_lengths, weight_rows = operands
    row_count, total, _ = cached.shape
    heads = final_query.shape[1] // HEAD
    positions = jnp.arange(total, dtype=jnp.int32)
    is_last = (positions[None, :] == (row_lengths - 1)[:, None])[:, None, :]
    query = final_query.reshape(row_count, heads, HEAD)
    scores = jnp.einsum("rgd,rld->rgl", query, cached[:, :, :HEAD], preferred_element_type=jnp.float32)
    new_score = jnp.einsum("rgd,rd->rg", query, new_pair[:, :HEAD], preferred_element_type=jnp.float32)
    scores = jnp.where(is_last, new_score[:, :, None], scores) * HEAD ** -0.5
    valid = (positions[None, :] < row_lengths[:, None])[:, None, :]
    scores = jnp.where(valid, scores, neg_big)
    weights = jnp.where(valid, jnp.exp(scores - jnp.max(scores, axis=-1, keepdims=True)), 0.0)
    rounded = weights.astype(jnp.bfloat16)
    old = jnp.where(is_last, jnp.zeros_like(rounded), rounded)
    new = jnp.sum(jnp.where(is_last, rounded.astype(jnp.float32), 0.0), axis=-1)
    mixed = jnp.einsum("rgl,rld->rgd", old, cached[:, :, HEAD:], preferred_element_type=jnp.float32)
    mixed = mixed + new[:, :, None] * new_pair[:, None, HEAD:].astype(jnp.float32)
    attended = (mixed / jnp.sum(weights, axis=-1)[..., None]).astype(jnp.bfloat16)
    return jnp.dot(attended.reshape(row_count, heads * HEAD), weight_rows, preferred_element_type=jnp.float32)


def shards(
    key_value_cache, new_kv, final_query, out_weight, lengths, block_plan, queries, output_gradient
):
    grp_index = lax.axis_index("grp")
    ctx_index = lax.axis_index("ctx")
    ctx_size = lax.axis_size("ctx")
    tp_size = lax.axis_size("tp")
    ring = ctx_size // 2
    z_index, column = ctx_index >> 1, ctx_index & 1
    core = lax.axis_index("tp") & 1

    def route(groups, move, stay=False):
        pairs = []
        for at in itertools.product(groups, range(ring), range(2), range(tp_size // 2), range(2)):
            to = move(*at)
            if stay or to != at:
                pairs.append(tuple((((g * ring + z) * 2 + h) * tp_size) + y * 2 + c for g, z, h, y, c in (at, to)))
        return pairs

    def sent(x, pairs):
        return lax.ppermute(x, ("grp", "ctx", "tp"), pairs)

    swap = route((1,), lambda g, z, h, y, c: (g, z, c, y, h))
    swap_all = route((1,), lambda g, z, h, y, c: (g, z, c, y, h), True)
    cores = route((0, 1), lambda g, z, h, y, c: (g, z, h, y, 1 - c))
    across = route((0,), lambda g, z, h, y, c: (1, z, c, y, h))

    cached = key_value_cache[0]
    row_count, total, width = cached.shape
    run = total // ring
    half = run // 2
    owner, *runs = finished_runs(lengths, z_index, cached, new_kv[0], ring)
    owner = owner[0]
    owner_z = owner >> 1
    distance = lax.rem(z_index + ring - owner_z, ring)

    def scatter_from(first):
        def scatter(parts):
            got = parts[0]
            for step in sorted(range(1, ring), key=lambda step: (-abs(step - ring // 2), -step)):
                pairs = [
                    (z * 2 + h, (z + step) % ring * 2 + h) for z in range(first, ring, classes) for h in range(2)
                ]
                arrived = lax.ppermute(parts[step], ("grp", "ctx"), pairs)
                got = jnp.where(distance == step, arrived, got)
            return got

        return scatter

    classes = ring // 2
    held = lax.switch(lax.rem(owner_z, classes), [scatter_from(first) for first in range(classes)], runs)

    stays = column == core
    query_rows = sent(queries[0], swap_all)
    gradient_rows = sent(output_gradient[0], swap)
    gradient_rows = jnp.where(stays, output_gradient[0], gradient_rows)
    landed = sent(held, across)
    landed, query_rows, gradient_rows, order = lax.optimization_barrier(
        (landed, query_rows, gradient_rows, jnp.argsort(block_plan, stable=True).astype(jnp.int32))
    )
    low, high = landed[:half], landed[half:]
    handed = sent(jnp.where(core == 0, high, low), cores)
    own = jnp.where(core == (owner & 1), jnp.where(core == 0, low, high), handed)
    columns = [list(range(h, ctx_size, 2)) for h in range(2)]

    def turned(x, step):
        return lax.ppermute(x, "ctx", [(z * 2 + h, (z + step) % ring * 2 + h) for z in range(ring) for h in range(2)])

    on, back, parts = own, own, [own]
    for _ in range(ring // 2 - 1):
        on, back = turned(on, 1), turned(back, -1)
        parts += [on, back]
    parts += [turned(on[:half // 2], 1), turned(back[half // 2:], -1)]
    mine = jnp.concatenate(parts, axis=0)
    other = sent(mine, cores)

    meta = jnp.stack([z_index * 2 + core, grp_index, core]).astype(jnp.int32)
    result_rows, kept, passed = attention(order, meta, mine, other, query_rows, gradient_rows)
    summed = (kept + sent(passed, cores).astype(jnp.float32)).astype(jnp.bfloat16)
    spread = lax.all_to_all(
        summed.reshape(ring, total // ctx_size, width), "ctx", 0, 0, axis_index_groups=columns
    )
    returned = sent(result_rows, swap)
    attn_out = jnp.where(stays, result_rows[0], returned[0])
    grad_query = jnp.where(stays, result_rows[1], returned[1])
    spread, attn_out, grad_query = lax.optimization_barrier((spread, attn_out, grad_query))
    grads = jnp.sum(spread.astype(jnp.float32), axis=0).astype(jnp.bfloat16)
    grad_pairs = sent(grads, swap_all)

    row_lengths = lax.dynamic_slice_in_dim(lengths, ctx_index * row_count, row_count)
    held_query, _ = lax.optimization_barrier((final_query[0], held))
    partial_out = lax.cond(
        grp_index == 0,
        decode_rows,
        lambda operands: jnp.zeros((row_count, out_weight.shape[2]), jnp.float32),
        (cached, new_kv[0], held_query, row_lengths, out_weight[0]),
    )
    partial_out = partial_out + sent(partial_out, cores)
    count = tp_size // 2
    onward = route((0,), lambda g, z, h, y, c: (g, z, h, (y + 1) % count, c))
    terms = [partial_out]
    for _ in range(count - 1):
        terms.append(sent(terms[-1], onward))
    y_index = lax.axis_index("tp") >> 1
    partial_out = jnp.zeros_like(partial_out)
    for y in range(count):
        back = (y_index - y) & (count - 1)
        partial_out = partial_out + sum(jnp.where(back == step, terms[step], 0.0) for step in range(count))
    decoded = partial_out.astype(jnp.bfloat16)
    return (decoded[None], attn_out[None], grad_query[None], grad_pairs[None])


def solution(mesh):
    return jax.shard_map(
        shards,
        mesh=mesh,
        in_specs=(
            P("grp", "ctx", None, "tp"),
            P("grp", "ctx", "tp"),
            P("grp", "ctx", "tp"),
            P("grp", "tp", None),
            P(),
            P(),
            P("grp", "ctx", "tp"),
            P("grp", "ctx", "tp"),
        ),
        out_specs=(
            P("grp", "ctx", None),
            P("grp", "ctx", "tp"),
            P("grp", "ctx", "tp"),
            P("grp", "ctx", "tp"),
        ),
        check_vma=False,
    )
```

```python
import functools
import itertools
import math

import jax
import jax.numpy as jnp
from jax import lax
from jax.experimental import pallas as pl
from jax.experimental.pallas import tpu as pltpu
from jax.sharding import PartitionSpec as P

HEAD = 128
TOKENS = 96
KEYS = 768
neg_big = -1e30


def attention_kernel(heads, blk, order_ref, meta_ref, *refs):
    mine_ref, other_ref, q_ref, do_ref, out_ref, keep_ref, send_ref, kv_ref, kt_s, vt_s, s_s, p_s, dk_s, dv_s, dq_s, o_s = refs
    total = kv_ref.shape[0]
    toks = q_ref.shape[0]
    gt, kc = TOKENS, KEYS
    rows = gt * heads
    sub = gt // blk
    me = meta_ref[0]
    learner = meta_ref[1]
    core = meta_ref[2]
    scale = HEAD ** -0.5
    factor = scale * math.log2(math.e)

    @pl.when(learner == 0)
    def _():
        out_ref[...] = jnp.zeros_like(out_ref)
        keep_ref[...] = jnp.zeros_like(keep_ref)
        send_ref[...] = jnp.zeros_like(send_ref)

    @pl.when(learner == 1)
    def _():
        half = toks
        ring = total // half // 2
        z = lax.div(me, 2)
        for r in range(ring):
            run = lax.rem(z + ring + (r // 2 if r % 2 == 0 else -(r + 1) // 2), ring)
            if r == ring - 1:
                run = lax.rem(z + ring // 2, ring)
            for ref, which in ((mine_ref, core), (other_ref, 1 - core)):
                start = pl.multiple_of((2 * run + which) * half, half)
                kv_ref[pl.ds(start, half), :] = ref[r * half:(r + 1) * half, :]

        for c in range(total // 256):
            part = pl.ds(c * 256, 256)
            kt_s[:, part] = kv_ref[part, :HEAD].T
            vt_s[:, part] = kv_ref[part, HEAD:].T
        dk_s[...] = jnp.zeros_like(dk_s)
        dv_s[...] = jnp.zeros_like(dv_s)

        def stacked(ref, base):
            return jnp.concatenate([ref[pl.ds(base, gt), h * HEAD:(h + 1) * HEAD] for h in range(heads)], axis=0)

        def spread(which, base, value):
            for h in range(heads):
                out_ref[which, pl.ds(base, gt), h * HEAD:(h + 1) * HEAD] = value[h * gt:(h + 1) * gt]

        def prepare(g):
            base = g * gt
            firsts = [order_ref[me * (toks // blk) + g * sub + s] * blk for s in range(sub)]
            lane = lax.rem(lax.broadcasted_iota(jnp.int32, (1, rows), 1), gt)
            pos = firsts[0] + lane
            for s in range(1, sub):
                pos = jnp.where(lane >= s * blk, firsts[s] + lane - s * blk, pos)
            full = lax.div(firsts[0] + 1, kc)
            last = lax.div(firsts[-1] + blk + kc - 1, kc)
            q = stacked(q_ref, base)
            o_s[g] = jnp.zeros_like(o_s[g])
            dq_s[g] = jnp.zeros_like(dq_s[g])
            return pos, full, last, q, q.T, stacked(do_ref, base).T

        def keys_of(c):
            return pl.ds(pl.multiple_of(c * kc, kc), kc)

        def scores(g, masked, c, m):
            pos, qt = state[g][0], state[g][4]
            s = jnp.dot(kv_ref[keys_of(c), :HEAD], qt, preferred_element_type=jnp.float32)
            if masked:
                kpos = c * kc + lax.broadcasted_iota(jnp.int32, (kc, rows), 0)
                s = jnp.where(kpos <= pos, s, neg_big)
            s_s[g, keys_of(c), :] = s
            return jnp.maximum(m, jnp.max(s.reshape(kc // 8, 8, rows), axis=0))

        def weigh(g, m, c, l):
            p = jnp.exp2((s_s[g, keys_of(c), :] - m) * factor)
            l = l + jnp.sum(p.reshape(kc // 8, 8, rows), axis=0)
            pb = p.astype(jnp.bfloat16)
            p_s[g, keys_of(c), :] = pb
            o_s[g] += jnp.dot(vt_s[:, keys_of(c)], pb, preferred_element_type=jnp.float32)
            return l

        def settle(g, l):
            inv = 1.0 / jnp.sum(l, axis=0, keepdims=True)
            ob = (o_s[g] * inv).astype(jnp.bfloat16)
            spread(0, g * gt, ob.T)
            dot_f = state[g][5].astype(jnp.float32)
            delta = jnp.sum(dot_f * ob.astype(jnp.float32), axis=0, keepdims=True) * inv
            dots = (dot_f * inv).astype(jnp.bfloat16)
            return delta, dots, dots.T

        def back(g, settled, c):
            delta, dots, dos = settled
            dp = jnp.dot(kv_ref[keys_of(c), HEAD:], dots, preferred_element_type=jnp.float32)
            pb = p_s[g, keys_of(c), :]
            ds = (pb.astype(jnp.float32) * (dp - delta)).astype(jnp.bfloat16)
            dv_s[keys_of(c), :] += jnp.dot(pb, dos, preferred_element_type=jnp.float32)
            dk_s[keys_of(c), :] += jnp.dot(ds, state[g][3], preferred_element_type=jnp.float32)
            dq_s[g] += jnp.dot(kt_s[:, keys_of(c)], ds, preferred_element_type=jnp.float32)

        def topmost(m):
            return jnp.max(m, axis=0, keepdims=True)

        state = [prepare(0), prepare(1)]
        full0, last0 = state[0][1:3]
        full1, last1 = state[1][1:3]
        low = jnp.full((8, rows), neg_big, jnp.float32)
        none = jnp.zeros((8, rows), jnp.float32)
        m0 = lax.fori_loop(0, full0, functools.partial(scores, 0, False), low)
        m0 = topmost(lax.fori_loop(full0, last0, functools.partial(scores, 0, True), m0))

        def both_forward(c, carry):
            return weigh(0, m0, c, carry[0]), scores(1, True, c, carry[1])

        l0, m1 = lax.fori_loop(0, last0, both_forward, (none, low))
        m1 = lax.fori_loop(last0, full1, functools.partial(scores, 1, False), m1)
        m1 = topmost(lax.fori_loop(jnp.maximum(last0, full1), last1, functools.partial(scores, 1, True), m1))
        settled0 = settle(0, l0)

        def both_ways(c, l):
            back(0, settled0, c)
            return weigh(1, m1, c, l)

        l1 = lax.fori_loop(0, last0, both_ways, none)
        l1 = lax.fori_loop(last0, last1, functools.partial(weigh, 1, m1), l1)
        settled1 = settle(1, l1)
        spread(1, 0, (dq_s[0] * scale).astype(jnp.bfloat16).T)

        def rest(c, _):
            back(1, settled1, c)
            return 0

        lax.fori_loop(0, last1, rest, 0)
        spread(1, gt, (dq_s[1] * scale).astype(jnp.bfloat16).T)

        per = toks // blk

        def put(parity, ref, i, _):
            shard = lax.div(i, per) * 2 + parity
            src = pl.ds(pl.multiple_of(order_ref[shard * per + lax.rem(i, per)] * blk, blk), blk)
            dst = pl.ds(pl.multiple_of(i * blk, blk), blk)
            ref[dst, :HEAD] = (dk_s[src, :] * scale).astype(ref.dtype)
            ref[dst, HEAD:] = dv_s[src, :].astype(ref.dtype)
            return 0

        lax.fori_loop(0, total // blk // 2, functools.partial(put, core, keep_ref), 0, unroll=8)
        lax.fori_loop(0, total // blk // 2, functools.partial(put, 1 - core, send_ref), 0, unroll=8)


def attention(order, meta, mine, other, q, do):
    total = mine.shape[0] * 2
    heads = q.shape[1] // HEAD
    rows = TOKENS * heads
    vmem = pl.BlockSpec(memory_space=pltpu.VMEM)
    smem = pl.BlockSpec(memory_space=pltpu.SMEM)
    return pl.pallas_call(
        functools.partial(attention_kernel, heads, total // order.shape[0]),
        out_shape=(
            jax.ShapeDtypeStruct((2,) + q.shape, jnp.bfloat16),
            jax.ShapeDtypeStruct((total // 2, 2 * HEAD), jnp.float32),
            jax.ShapeDtypeStruct((total // 2, 2 * HEAD), jnp.bfloat16),
        ),
        in_specs=[smem, smem] + [vmem] * 4,
        out_specs=(vmem, vmem, vmem),
        scratch_shapes=[
            pltpu.VMEM((total, 2 * HEAD), jnp.bfloat16),
            pltpu.VMEM((HEAD, total), jnp.bfloat16),
            pltpu.VMEM((HEAD, total), jnp.bfloat16),
            pltpu.VMEM((2, total, rows), jnp.float32),
            pltpu.VMEM((2, total, rows), jnp.bfloat16),
            pltpu.VMEM((total, HEAD), jnp.float32),
            pltpu.VMEM((total, HEAD), jnp.float32),
            pltpu.VMEM((2, HEAD, rows), jnp.float32),
            pltpu.VMEM((2, HEAD, rows), jnp.float32),
        ],
        compiler_params=pltpu.CompilerParams(vmem_limit_bytes=52 * 2**20),
    )(order, meta, mine, other, q, do)


def runs_kernel(lengths_ref, z_ref, cached_ref, new_ref, owner_ref, *refs):
    run_refs, sems = refs[:-1], refs[-1]
    ring = len(run_refs)
    run = run_refs[0].shape[0]
    row_count, total, _ = cached_ref.shape
    finished = jnp.int32(0)
    for r in range(lengths_ref.shape[0]):
        finished = jnp.where(lengths_ref[r] == total, r, finished)
    picked = lax.rem(finished, row_count)
    owner_ref[0] = lax.div(finished, row_count)
    copies = []
    for step, ref in enumerate(run_refs):
        start = pl.multiple_of(lax.rem(z_ref[0] + step, ring) * run, run)
        copies.append(pltpu.make_async_copy(cached_ref.at[picked, pl.ds(start, run)], ref, sems.at[step]))
    for copy in copies:
        copy.start()
    new_row = new_ref[0:1, :]
    for r in range(1, row_count):
        new_row = jnp.where(picked == r, new_ref[r:r + 1, :], new_row)
    for copy in copies:
        copy.wait()
    for step, ref in enumerate(run_refs):
        @pl.when(lax.rem(z_ref[0] + step, ring) == ring - 1)
        def _(ref=ref):
            at = lax.broadcasted_iota(jnp.int32, (16, ref.shape[1]), 0)
            tail = pl.ds(run - 16, 16)
            ref[tail, :] = jnp.where(at == 15, new_row, ref[tail, :])


def finished_runs(lengths, z_index, cached, new_pairs, ring):
    total, width = cached.shape[1:]
    vmem = pl.BlockSpec(memory_space=pltpu.VMEM)
    smem = pl.BlockSpec(memory_space=pltpu.SMEM)
    return pl.pallas_call(
        runs_kernel,
        out_shape=[jax.ShapeDtypeStruct((1,), jnp.int32)]
        + [jax.ShapeDtypeStruct((total // ring, width), cached.dtype)] * ring,
        in_specs=[smem, smem, pl.BlockSpec(memory_space=pl.ANY), vmem],
        out_specs=[smem] + [vmem] * ring,
        scratch_shapes=[pltpu.SemaphoreType.DMA((ring,))],
        compiler_params=pltpu.CompilerParams(vmem_limit_bytes=16 * 2**20),
    )(lengths, z_index.reshape(1), cached, new_pairs)


def decode_rows(operands):
    cached, new_pair, final_query, row_lengths, weight_rows = operands
    row_count, total, _ = cached.shape
    heads = final_query.shape[1] // HEAD
    positions = jnp.arange(total, dtype=jnp.int32)
    is_last = (positions[None, :] == (row_lengths - 1)[:, None])[:, None, :]
    query = final_query.reshape(row_count, heads, HEAD)
    scores = jnp.einsum("rgd,rld->rgl", query, cached[:, :, :HEAD], preferred_element_type=jnp.float32)
    new_score = jnp.einsum("rgd,rd->rg", query, new_pair[:, :HEAD], preferred_element_type=jnp.float32)
    scores = jnp.where(is_last, new_score[:, :, None], scores) * HEAD ** -0.5
    valid = (positions[None, :] < row_lengths[:, None])[:, None, :]
    scores = jnp.where(valid, scores, neg_big)
    weights = jnp.where(valid, jnp.exp(scores - jnp.max(scores, axis=-1, keepdims=True)), 0.0)
    rounded = weights.astype(jnp.bfloat16)
    old = jnp.where(is_last, jnp.zeros_like(rounded), rounded)
    new = jnp.sum(jnp.where(is_last, rounded.astype(jnp.float32), 0.0), axis=-1)
    mixed = jnp.einsum("rgl,rld->rgd", old, cached[:, :, HEAD:], preferred_element_type=jnp.float32)
    mixed = mixed + new[:, :, None] * new_pair[:, None, HEAD:].astype(jnp.float32)
    attended = (mixed / jnp.sum(weights, axis=-1)[..., None]).astype(jnp.bfloat16)
    return jnp.dot(attended.reshape(row_count, heads * HEAD), weight_rows, preferred_element_type=jnp.float32)


def shards(
    key_value_cache, new_kv, final_query, out_weight, lengths, block_plan, queries, output_gradient
):
    grp_index = lax.axis_index("grp")
    ctx_index = lax.axis_index("ctx")
    ctx_size = lax.axis_size("ctx")
    tp_size = lax.axis_size("tp")
    ring = ctx_size // 2
    z_index, column = ctx_index >> 1, ctx_index & 1
    core = lax.axis_index("tp") & 1

    def route(groups, move, stay=False):
        pairs = []
        for at in itertools.product(groups, range(ring), range(2), range(tp_size // 2), range(2)):
            to = move(*at)
            if stay or to != at:
                pairs.append(tuple((((g * ring + z) * 2 + h) * tp_size) + y * 2 + c for g, z, h, y, c in (at, to)))
        return pairs

    def sent(x, pairs):
        return lax.ppermute(x, ("grp", "ctx", "tp"), pairs)

    swap = route((1,), lambda g, z, h, y, c: (g, z, c, y, h))
    swap_all = route((1,), lambda g, z, h, y, c: (g, z, c, y, h), True)
    cores = route((0, 1), lambda g, z, h, y, c: (g, z, h, y, 1 - c))
    across = route((0,), lambda g, z, h, y, c: (1, z, c, y, h))

    cached = key_value_cache[0]
    row_count, total, width = cached.shape
    run = total // ring
    half = run // 2
    owner, *runs = finished_runs(lengths, z_index, cached, new_kv[0], ring)
    owner = owner[0]
    owner_z = owner >> 1
    distance = lax.rem(z_index + ring - owner_z, ring)

    def scatter_from(first):
        def scatter(parts):
            got = parts[0]
            for step in sorted(range(1, ring), key=lambda step: (-abs(step - ring // 2), -step)):
                pairs = [
                    (z * 2 + h, (z + step) % ring * 2 + h) for z in range(first, ring, classes) for h in range(2)
                ]
                arrived = lax.ppermute(parts[step], ("grp", "ctx"), pairs)
                got = jnp.where(distance == step, arrived, got)
            return got

        return scatter

    classes = ring // 2
    held = lax.switch(lax.rem(owner_z, classes), [scatter_from(first) for first in range(classes)], runs)

    stays = column == core
    query_rows = sent(queries[0], swap_all)
    gradient_rows = sent(output_gradient[0], swap)
    gradient_rows = jnp.where(stays, output_gradient[0], gradient_rows)
    landed = sent(held, across)
    landed, query_rows, gradient_rows, order = lax.optimization_barrier(
        (landed, query_rows, gradient_rows, jnp.argsort(block_plan, stable=True).astype(jnp.int32))
    )
    low, high = landed[:half], landed[half:]
    handed = sent(jnp.where(core == 0, high, low), cores)
    own = jnp.where(core == (owner & 1), jnp.where(core == 0, low, high), handed)
    columns = [list(range(h, ctx_size, 2)) for h in range(2)]

    def turned(x, step):
        return lax.ppermute(x, "ctx", [(z * 2 + h, (z + step) % ring * 2 + h) for z in range(ring) for h in range(2)])

    on, back, parts = own, own, [own]
    for _ in range(ring // 2 - 1):
        on, back = turned(on, 1), turned(back, -1)
        parts += [on, back]
    parts += [turned(on[:half // 2], 1), turned(back[half // 2:], -1)]
    mine = jnp.concatenate(parts, axis=0)
    other = sent(mine, cores)

    meta = jnp.stack([z_index * 2 + core, grp_index, core]).astype(jnp.int32)
    result_rows, kept, passed = attention(order, meta, mine, other, query_rows, gradient_rows)
    summed = (kept + sent(passed, cores).astype(jnp.float32)).astype(jnp.bfloat16)
    spread = lax.all_to_all(
        summed.reshape(ring, total // ctx_size, width), "ctx", 0, 0, axis_index_groups=columns
    )
    returned = sent(result_rows, swap)
    attn_out = jnp.where(stays, result_rows[0], returned[0])
    grad_query = jnp.where(stays, result_rows[1], returned[1])
    spread, attn_out, grad_query = lax.optimization_barrier((spread, attn_out, grad_query))
    grads = jnp.sum(spread.astype(jnp.float32), axis=0).astype(jnp.bfloat16)
    grad_pairs = sent(grads, swap_all)

    row_lengths = lax.dynamic_slice_in_dim(lengths, ctx_index * row_count, row_count)
    held_query, _ = lax.optimization_barrier((final_query[0], held))
    partial_out = lax.cond(
        grp_index == 0,
        decode_rows,
        lambda operands: jnp.zeros((row_count, out_weight.shape[2]), jnp.float32),
        (cached, new_kv[0], held_query, row_lengths, out_weight[0]),
    )
    partial_out = partial_out + sent(partial_out, cores)
    count = tp_size // 2
    onward = route((0,), lambda g, z, h, y, c: (g, z, h, (y + 1) % count, c))
    terms = [partial_out]
    for _ in range(count - 1):
        terms.append(sent(terms[-1], onward))
    y_index = lax.axis_index("tp") >> 1
    partial_out = jnp.zeros_like(partial_out)
    for y in range(count):
        back = (y_index - y) & (count - 1)
        partial_out = partial_out + sum(jnp.where(back == step, terms[step], 0.0) for step in range(count))
    decoded = partial_out.astype(jnp.bfloat16)
    return (decoded[None], attn_out[None], grad_query[None], grad_pairs[None])


def solution(mesh):
    return jax.shard_map(
        shards,
        mesh=mesh,
        in_specs=(
            P("grp", "ctx", None, "tp"),
            P("grp", "ctx", "tp"),
            P("grp", "ctx", "tp"),
            P("grp", "tp", None),
            P(),
            P(),
            P("grp", "ctx", "tp"),
            P("grp", "ctx", "tp"),
        ),
        out_specs=(
            P("grp", "ctx", None),
            P("grp", "ctx", "tp"),
            P("grp", "ctx", "tp"),
            P("grp", "ctx", "tp"),
        ),
        check_vma=False,
    )
```

```python
import functools
import itertools
import math

import jax
import jax.numpy as jnp
from jax import lax
from jax.experimental import pallas as pl
from jax.experimental.pallas import tpu as pltpu
from jax.sharding import PartitionSpec as P

HEAD = 128
TOKENS = 96
KEYS = 768
neg_big = -1e30


def attention_kernel(heads, blk, order_ref, meta_ref, *refs):
    mine_ref, other_ref, q_ref, do_ref, out_ref, keep_ref, send_ref, kv_ref, kt_s, vt_s, s_s, p_s, dk_s, dv_s, dq_s, o_s = refs
    total = kv_ref.shape[0]
    toks = q_ref.shape[0]
    gt, kc = TOKENS, KEYS
    rows = gt * heads
    sub = gt // blk
    me = meta_ref[0]
    learner = meta_ref[1]
    core = meta_ref[2]
    scale = HEAD ** -0.5
    factor = scale * math.log2(math.e)

    @pl.when(learner == 0)
    def _():
        out_ref[...] = jnp.zeros_like(out_ref)
        keep_ref[...] = jnp.zeros_like(keep_ref)
        send_ref[...] = jnp.zeros_like(send_ref)

    @pl.when(learner == 1)
    def _():
        half = toks
        ring = total // half // 2
        z = lax.div(me, 2)
        for r in range(ring):
            run = lax.rem(z + ring + (r // 2 if r % 2 == 0 else -(r + 1) // 2), ring)
            if r == ring - 1:
                run = lax.rem(z + ring // 2, ring)
            for ref, which in ((mine_ref, core), (other_ref, 1 - core)):
                start = pl.multiple_of((2 * run + which) * half, half)
                kv_ref[pl.ds(start, half), :] = ref[r * half:(r + 1) * half, :]

        for c in range(total // 256):
            part = pl.ds(c * 256, 256)
            kt_s[:, part] = kv_ref[part, :HEAD].T
            vt_s[:, part] = kv_ref[part, HEAD:].T
        dk_s[...] = jnp.zeros_like(dk_s)
        dv_s[...] = jnp.zeros_like(dv_s)

        def stacked(ref, base):
            return jnp.concatenate([ref[pl.ds(base, gt), h * HEAD:(h + 1) * HEAD] for h in range(heads)], axis=0)

        def spread(which, base, value):
            for h in range(heads):
                out_ref[which, pl.ds(base, gt), h * HEAD:(h + 1) * HEAD] = value[h * gt:(h + 1) * gt]

        def prepare(g):
            base = g * gt
            firsts = [order_ref[me * (toks // blk) + g * sub + s] * blk for s in range(sub)]
            lane = lax.rem(lax.broadcasted_iota(jnp.int32, (1, rows), 1), gt)
            pos = firsts[0] + lane
            for s in range(1, sub):
                pos = jnp.where(lane >= s * blk, firsts[s] + lane - s * blk, pos)
            full = lax.div(firsts[0] + 1, kc)
            last = lax.div(firsts[-1] + blk + kc - 1, kc)
            q = stacked(q_ref, base)
            o_s[g] = jnp.zeros_like(o_s[g])
            dq_s[g] = jnp.zeros_like(dq_s[g])
            return pos, full, last, q, q.T, stacked(do_ref, base).T

        def keys_of(c):
            return pl.ds(pl.multiple_of(c * kc, kc), kc)

        def scores(g, masked, c, m):
            pos, qt = state[g][0], state[g][4]
            s = jnp.dot(kv_ref[keys_of(c), :HEAD], qt, preferred_element_type=jnp.float32)
            if masked:
                kpos = c * kc + lax.broadcasted_iota(jnp.int32, (kc, rows), 0)
                s = jnp.where(kpos <= pos, s, neg_big)
            s_s[keys_of(c), :] = s
            return jnp.maximum(m, jnp.max(s.reshape(kc // 8, 8, rows), axis=0))

        def weigh(g, m, c, l):
            p = jnp.exp2((s_s[keys_of(c), :] - m) * factor)
            l = l + jnp.sum(p.reshape(kc // 8, 8, rows), axis=0)
            pb = p.astype(jnp.bfloat16)
            p_s[keys_of(c), :] = pb
            o_s[g] += jnp.dot(vt_s[:, keys_of(c)], pb, preferred_element_type=jnp.float32)
            return l

        def settle(g, l):
            inv = 1.0 / jnp.sum(l, axis=0, keepdims=True)
            ob = (o_s[g] * inv).astype(jnp.bfloat16)
            spread(0, g * gt, ob.T)
            dot_f = state[g][5].astype(jnp.float32)
            delta = jnp.sum(dot_f * ob.astype(jnp.float32), axis=0, keepdims=True) * inv
            dots = (dot_f * inv).astype(jnp.bfloat16)
            return delta, dots, dots.T

        def back(g, settled, c):
            delta, dots, dos = settled
            dp = jnp.dot(kv_ref[keys_of(c), HEAD:], dots, preferred_element_type=jnp.float32)
            pb = p_s[keys_of(c), :]
            ds = (pb.astype(jnp.float32) * (dp - delta)).astype(jnp.bfloat16)
            dv_s[keys_of(c), :] += jnp.dot(pb, dos, preferred_element_type=jnp.float32)
            dk_s[keys_of(c), :] += jnp.dot(ds, state[g][3], preferred_element_type=jnp.float32)
            dq_s[g] += jnp.dot(kt_s[:, keys_of(c)], ds, preferred_element_type=jnp.float32)

        def topmost(m):
            return jnp.max(m, axis=0, keepdims=True)

        state = [prepare(0), prepare(1)]
        full0, last0 = state[0][1:3]
        full1, last1 = state[1][1:3]
        low = jnp.full((8, rows), neg_big, jnp.float32)
        none = jnp.zeros((8, rows), jnp.float32)
        m0 = lax.fori_loop(0, full0, functools.partial(scores, 0, False), low)
        m0 = topmost(lax.fori_loop(full0, last0, functools.partial(scores, 0, True), m0))

        def both_forward(c, carry):
            return weigh(0, m0, c, carry[0]), scores(1, True, c, carry[1])

        l0, m1 = lax.fori_loop(0, last0, both_forward, (none, low))
        m1 = lax.fori_loop(last0, full1, functools.partial(scores, 1, False), m1)
        m1 = topmost(lax.fori_loop(jnp.maximum(last0, full1), last1, functools.partial(scores, 1, True), m1))
        settled0 = settle(0, l0)

        def both_ways(c, l):
            back(0, settled0, c)
            return weigh(1, m1, c, l)

        l1 = lax.fori_loop(0, last0, both_ways, none)
        l1 = lax.fori_loop(last0, last1, functools.partial(weigh, 1, m1), l1)
        settled1 = settle(1, l1)
        spread(1, 0, (dq_s[0] * scale).astype(jnp.bfloat16).T)

        def rest(c, _):
            back(1, settled1, c)
            return 0

        lax.fori_loop(0, last1, rest, 0)
        spread(1, gt, (dq_s[1] * scale).astype(jnp.bfloat16).T)

        per = toks // blk

        def put(parity, ref, i, _):
            shard = lax.div(i, per) * 2 + parity
            src = pl.ds(pl.multiple_of(order_ref[shard * per + lax.rem(i, per)] * blk, blk), blk)
            dst = pl.ds(pl.multiple_of(i * blk, blk), blk)
            ref[dst, :HEAD] = (dk_s[src, :] * scale).astype(ref.dtype)
            ref[dst, HEAD:] = dv_s[src, :].astype(ref.dtype)
            return 0

        lax.fori_loop(0, total // blk // 2, functools.partial(put, core, keep_ref), 0, unroll=8)
        lax.fori_loop(0, total // blk // 2, functools.partial(put, 1 - core, send_ref), 0, unroll=8)


def attention(order, meta, mine, other, q, do):
    total = mine.shape[0] * 2
    heads = q.shape[1] // HEAD
    rows = TOKENS * heads
    vmem = pl.BlockSpec(memory_space=pltpu.VMEM)
    smem = pl.BlockSpec(memory_space=pltpu.SMEM)
    return pl.pallas_call(
        functools.partial(attention_kernel, heads, total // order.shape[0]),
        out_shape=(
            jax.ShapeDtypeStruct((2,) + q.shape, jnp.bfloat16),
            jax.ShapeDtypeStruct((total // 2, 2 * HEAD), jnp.float32),
            jax.ShapeDtypeStruct((total // 2, 2 * HEAD), jnp.bfloat16),
        ),
        in_specs=[smem, smem] + [vmem] * 4,
        out_specs=(vmem, vmem, vmem),
        scratch_shapes=[
            pltpu.VMEM((total, 2 * HEAD), jnp.bfloat16),
            pltpu.VMEM((HEAD, total), jnp.bfloat16),
            pltpu.VMEM((HEAD, total), jnp.bfloat16),
            pltpu.VMEM((total, rows), jnp.float32),
            pltpu.VMEM((total, rows), jnp.bfloat16),
            pltpu.VMEM((total, HEAD), jnp.float32),
            pltpu.VMEM((total, HEAD), jnp.float32),
            pltpu.VMEM((2, HEAD, rows), jnp.float32),
            pltpu.VMEM((2, HEAD, rows), jnp.float32),
        ],
        compiler_params=pltpu.CompilerParams(vmem_limit_bytes=40 * 2**20),
    )(order, meta, mine, other, q, do)


def runs_kernel(lengths_ref, z_ref, cached_ref, new_ref, owner_ref, *refs):
    run_refs, sems = refs[:-1], refs[-1]
    ring = len(run_refs)
    run = run_refs[0].shape[0]
    row_count, total, _ = cached_ref.shape
    finished = jnp.int32(0)
    for r in range(lengths_ref.shape[0]):
        finished = jnp.where(lengths_ref[r] == total, r, finished)
    picked = lax.rem(finished, row_count)
    owner_ref[0] = lax.div(finished, row_count)
    copies = []
    for step, ref in enumerate(run_refs):
        start = pl.multiple_of(lax.rem(z_ref[0] + step, ring) * run, run)
        copies.append(pltpu.make_async_copy(cached_ref.at[picked, pl.ds(start, run)], ref, sems.at[step]))
    for copy in copies:
        copy.start()
    new_row = new_ref[0:1, :]
    for r in range(1, row_count):
        new_row = jnp.where(picked == r, new_ref[r:r + 1, :], new_row)
    for copy in copies:
        copy.wait()
    for step, ref in enumerate(run_refs):
        @pl.when(lax.rem(z_ref[0] + step, ring) == ring - 1)
        def _(ref=ref):
            at = lax.broadcasted_iota(jnp.int32, (16, ref.shape[1]), 0)
            tail = pl.ds(run - 16, 16)
            ref[tail, :] = jnp.where(at == 15, new_row, ref[tail, :])


def finished_runs(lengths, z_index, cached, new_pairs, ring):
    total, width = cached.shape[1:]
    vmem = pl.BlockSpec(memory_space=pltpu.VMEM)
    smem = pl.BlockSpec(memory_space=pltpu.SMEM)
    return pl.pallas_call(
        runs_kernel,
        out_shape=[jax.ShapeDtypeStruct((1,), jnp.int32)]
        + [jax.ShapeDtypeStruct((total // ring, width), cached.dtype)] * ring,
        in_specs=[smem, smem, pl.BlockSpec(memory_space=pl.ANY), vmem],
        out_specs=[smem] + [vmem] * ring,
        scratch_shapes=[pltpu.SemaphoreType.DMA((ring,))],
        compiler_params=pltpu.CompilerParams(vmem_limit_bytes=16 * 2**20),
    )(lengths, z_index.reshape(1), cached, new_pairs)


def decode_rows(operands):
    cached, new_pair, final_query, row_lengths, weight_rows = operands
    row_count, total, _ = cached.shape
    heads = final_query.shape[1] // HEAD
    positions = jnp.arange(total, dtype=jnp.int32)
    is_last = (positions[None, :] == (row_lengths - 1)[:, None])[:, None, :]
    query = final_query.reshape(row_count, heads, HEAD)
    scores = jnp.einsum("rgd,rld->rgl", query, cached[:, :, :HEAD], preferred_element_type=jnp.float32)
    new_score = jnp.einsum("rgd,rd->rg", query, new_pair[:, :HEAD], preferred_element_type=jnp.float32)
    scores = jnp.where(is_last, new_score[:, :, None], scores) * HEAD ** -0.5
    valid = (positions[None, :] < row_lengths[:, None])[:, None, :]
    scores = jnp.where(valid, scores, neg_big)
    weights = jnp.where(valid, jnp.exp(scores - jnp.max(scores, axis=-1, keepdims=True)), 0.0)
    rounded = weights.astype(jnp.bfloat16)
    old = jnp.where(is_last, jnp.zeros_like(rounded), rounded)
    new = jnp.sum(jnp.where(is_last, rounded.astype(jnp.float32), 0.0), axis=-1)
    mixed = jnp.einsum("rgl,rld->rgd", old, cached[:, :, HEAD:], preferred_element_type=jnp.float32)
    mixed = mixed + new[:, :, None] * new_pair[:, None, HEAD:].astype(jnp.float32)
    attended = (mixed / jnp.sum(weights, axis=-1)[..., None]).astype(jnp.bfloat16)
    return jnp.dot(attended.reshape(row_count, heads * HEAD), weight_rows, preferred_element_type=jnp.float32)


def shards(
    key_value_cache, new_kv, final_query, out_weight, lengths, block_plan, queries, output_gradient
):
    grp_index = lax.axis_index("grp")
    ctx_index = lax.axis_index("ctx")
    ctx_size = lax.axis_size("ctx")
    tp_size = lax.axis_size("tp")
    ring = ctx_size // 2
    z_index, column = ctx_index >> 1, ctx_index & 1
    core = lax.axis_index("tp") & 1

    def route(groups, move, stay=False):
        pairs = []
        for at in itertools.product(groups, range(ring), range(2), range(tp_size // 2), range(2)):
            to = move(*at)
            if stay or to != at:
                pairs.append(tuple((((g * ring + z) * 2 + h) * tp_size) + y * 2 + c for g, z, h, y, c in (at, to)))
        return pairs

    def sent(x, pairs):
        return lax.ppermute(x, ("grp", "ctx", "tp"), pairs)

    swap = route((1,), lambda g, z, h, y, c: (g, z, c, y, h))
    swap_all = route((1,), lambda g, z, h, y, c: (g, z, c, y, h), True)
    cores = route((0, 1), lambda g, z, h, y, c: (g, z, h, y, 1 - c))
    across = route((0,), lambda g, z, h, y, c: (1, z, c, y, h))

    cached = key_value_cache[0]
    row_count, total, width = cached.shape
    run = total // ring
    half = run // 2
    owner, *runs = finished_runs(lengths, z_index, cached, new_kv[0], ring)
    owner = owner[0]
    owner_z = owner >> 1
    distance = lax.rem(z_index + ring - owner_z, ring)

    def scatter_from(first):
        def scatter(parts):
            got = parts[0]
            for step in sorted(range(1, ring), key=lambda step: (-abs(step - ring // 2), -step)):
                pairs = [
                    (z * 2 + h, (z + step) % ring * 2 + h) for z in range(first, ring, classes) for h in range(2)
                ]
                arrived = lax.ppermute(parts[step], ("grp", "ctx"), pairs)
                got = jnp.where(distance == step, arrived, got)
            return got

        return scatter

    classes = ring // 2
    held = lax.switch(lax.rem(owner_z, classes), [scatter_from(first) for first in range(classes)], runs)

    stays = column == core
    query_rows = sent(queries[0], swap_all)
    gradient_rows = sent(output_gradient[0], swap)
    gradient_rows = jnp.where(stays, output_gradient[0], gradient_rows)
    landed = sent(held, across)
    landed, query_rows, gradient_rows, order = lax.optimization_barrier(
        (landed, query_rows, gradient_rows, jnp.argsort(block_plan, stable=True).astype(jnp.int32))
    )
    low, high = landed[:half], landed[half:]
    handed = sent(jnp.where(core == 0, high, low), cores)
    own = jnp.where(core == (owner & 1), jnp.where(core == 0, low, high), handed)
    columns = [list(range(h, ctx_size, 2)) for h in range(2)]

    def turned(x, step):
        return lax.ppermute(x, "ctx", [(z * 2 + h, (z + step) % ring * 2 + h) for z in range(ring) for h in range(2)])

    on, back, parts = own, own, [own]
    for _ in range(ring // 2 - 1):
        on, back = turned(on, 1), turned(back, -1)
        parts += [on, back]
    parts += [turned(on[:half // 2], 1), turned(back[half // 2:], -1)]
    mine = jnp.concatenate(parts, axis=0)
    other = sent(mine, cores)

    meta = jnp.stack([z_index * 2 + core, grp_index, core]).astype(jnp.int32)
    result_rows, kept, passed = attention(order, meta, mine, other, query_rows, gradient_rows)
    summed = (kept + sent(passed, cores).astype(jnp.float32)).astype(jnp.bfloat16)
    spread = lax.all_to_all(
        summed.reshape(ring, total // ctx_size, width), "ctx", 0, 0, axis_index_groups=columns
    )
    returned = sent(result_rows, swap)
    attn_out = jnp.where(stays, result_rows[0], returned[0])
    grad_query = jnp.where(stays, result_rows[1], returned[1])
    spread, attn_out, grad_query = lax.optimization_barrier((spread, attn_out, grad_query))
    grads = jnp.sum(spread.astype(jnp.float32), axis=0).astype(jnp.bfloat16)
    grad_pairs = sent(grads, swap_all)

    row_lengths = lax.dynamic_slice_in_dim(lengths, ctx_index * row_count, row_count)
    held_query, _ = lax.optimization_barrier((final_query[0], held))
    partial_out = lax.cond(
        grp_index == 0,
        decode_rows,
        lambda operands: jnp.zeros((row_count, out_weight.shape[2]), jnp.float32),
        (cached, new_kv[0], held_query, row_lengths, out_weight[0]),
    )
    partial_out = partial_out + sent(partial_out, cores)
    count = tp_size // 2
    onward = route((0,), lambda g, z, h, y, c: (g, z, h, (y + 1) % count, c))
    terms = [partial_out]
    for _ in range(count - 1):
        terms.append(sent(terms[-1], onward))
    y_index = lax.axis_index("tp") >> 1
    partial_out = jnp.zeros_like(partial_out)
    for y in range(count):
        back = (y_index - y) & (count - 1)
        partial_out = partial_out + sum(jnp.where(back == step, terms[step], 0.0) for step in range(count))
    decoded = partial_out.astype(jnp.bfloat16)
    return (decoded[None], attn_out[None], grad_query[None], grad_pairs[None])


def solution(mesh):
    return jax.shard_map(
        shards,
        mesh=mesh,
        in_specs=(
            P("grp", "ctx", None, "tp"),
            P("grp", "ctx", "tp"),
            P("grp", "ctx", "tp"),
            P("grp", "tp", None),
            P(),
            P(),
            P("grp", "ctx", "tp"),
            P("grp", "ctx", "tp"),
        ),
        out_specs=(
            P("grp", "ctx", None),
            P("grp", "ctx", "tp"),
            P("grp", "ctx", "tp"),
            P("grp", "ctx", "tp"),
        ),
        check_vma=False,
    )
```
